256 devices in a mesh: kx: 8 (over x, z_lo), kyz: 32 (over z_hi, y, core).
Axes of the slice: x: 4, y: 4, z: 8 (z_hi: 4, z_lo: 2; z = z_hi * 2 + z_lo), core: 2. Of those that a mesh axis runs over, the one named last changes fastest.
Arguments:
- intersections: float32 [8, 32, 2, 2, 6, 2, 128, 128], P('kx', 'kyz'), may hold values from -1.2 to 1.2
- rotations: float32 [8, 32, 2, 2, 2, 128, 128], P('kx', 'kyz'), may hold values from -0.2 to 1.2
- offsets: int32 [6, 3], replicated, may hold values from -1 to 1, as said below
- weights: float32 [6], replicated, may hold values from 0.3 to 1.5
- basis: float32 [3, 3], replicated, may hold values from -3 to 3
Outputs:
- gradient: float32 [8, 32, 2, 2, 2, 128, 128], P('kx', 'kyz')
- centres: float32 [3, 128], replicated
- spread: float32 [], replicated
The draws below stay inside these ranges and needn't reach their ends.
Inputs may be any that keep to these rules, and one draw needn't show every extreme that they name: `offsets`: each row is a step of -1, 0 or 1 along kx, ky and kz; no row is zero, no two rows are equal or opposite, and the unit steps along kx, ky and kz are among the rows.
All inputs are finite; a program needn't handle non-finite values.
Results may differ from the reference program's by a relative error of at most 0.0003.
Values sent between devices are 32-bit elements; how exact they have to be, the bound alone decides.
No kernel may reach another device: no remote copies, remote signals or barrier semaphores. Data moves between devices by JAX's collectives and lax.ppermute only.
A program may use at most 128 MiB of HBM per device.

```python
import math
import jax
import jax.numpy as jnp
import numpy as np
from jax import lax

J = 128
NB = 6
KZB = 4
NKX = 8
NKY = 16
NKZ = 8
NK = 1024


unit_steps = np.array([[1, 0, 0], [0, 1, 0], [0, 0, 1]])


diagonal_steps = np.array([[1, 1, 0], [1, -1, 0], [1, 0, 1], [1, 0, -1], [0, 1, 1], [0, 1, -1], [1, 1, 1], [1, 1, -1], [1, -1, 1], [1, -1, -1]])


def step_table(key):
    picked = jax.random.permutation(jax.random.fold_in(key, 11), 10)[:3]
    rows = jnp.concatenate([jnp.asarray(unit_steps, jnp.int32), jnp.asarray(diagonal_steps, jnp.int32)[picked]], 0)
    order = jax.random.permutation(jax.random.fold_in(key, 12), 6)
    return rows[order]


def draw_offsets(key, part):
    return step_table(key)


def draw_intersections(key, part):
    steps = step_table(key)
    key = jax.random.fold_in(key, 5)
    keys = jax.random.split(key, 4)
    bricks = NKY * NKZ // 4
    lead = (NKX, bricks, 2, 2, NB)
    radius = jax.random.uniform(keys[0], lead + (J,), jnp.float32, 0.7, 1.0)
    centre = jax.random.uniform(keys[1], (3, J), jnp.float32, -0.6, 0.6)
    fsteps = steps.astype(jnp.float32)
    base = -(fsteps[:, 0:1] * centre[0] + fsteps[:, 1:2] * centre[1] + fsteps[:, 2:3] * centre[2])
    place = (jnp.arange(NKX)[:, None] * bricks + jnp.arange(bricks)[None, :]).astype(jnp.float32) / (NKX * bricks - 1)
    amplitude = 0.15 + 0.35 * place
    noise = jax.random.uniform(keys[2], lead + (J,), jnp.float32, -1.0, 1.0)
    angle = base + amplitude[:, :, None, None, None, None] * noise
    scale = 0.3 / math.sqrt(J)
    rest = jax.random.truncated_normal(keys[3], -2.5, 2.5, lead + (2, J, J), jnp.float32) * scale
    eye = jnp.eye(J, dtype=jnp.float32)
    real_part = rest[..., 0, :, :] + eye * (radius * jnp.cos(angle))[..., None, :]
    imag_part = rest[..., 1, :, :] + eye * (radius * jnp.sin(angle))[..., None, :]
    return jnp.stack([real_part, imag_part], axis=-3)


def draw_rotations(key, part):
    key = jax.random.fold_in(key, 7)
    bricks = NKY * NKZ // 4
    shape = (NKX, bricks, 2, 2, 2, J, J)
    rest = jax.random.truncated_normal(key, -2.5, 2.5, shape, jnp.float32) * (0.25 / math.sqrt(J))
    eye = jnp.eye(J, dtype=jnp.float32)
    return jnp.stack([rest[..., 0, :, :] + eye, rest[..., 1, :, :]], axis=-3)


def scatter_about(stream_key, dims, deviation, limit, held_as=jnp.bfloat16):
    return jnp.clip(deviation * jax.random.normal(stream_key, dims, jnp.float32), -limit, limit).astype(held_as)


def setup_inputs(seed: int = 0) -> dict:
    streams_of = jax.random.split(jax.random.key(seed), 6)
    return {
        "intersections": draw_intersections(jax.random.fold_in(streams_of[5], 71), 0),
        "rotations": draw_rotations(jax.random.fold_in(streams_of[5], 71), 0),
        "offsets": draw_offsets(jax.random.fold_in(streams_of[5], 71), 0),
        "weights": jnp.clip(jnp.exp(jax.random.uniform(streams_of[3], (NB,), jnp.float32, math.log(0.3), math.log(1.5))), 0.3, 1.5),
        "basis": scatter_about(streams_of[4], (3, 3), 0.7, 3.0, jnp.float32),
    }


highest = lax.Precision.HIGHEST


def brick_order():
    return jnp.array([0, 1, 3, 2], dtype=jnp.int32)


def to_grid(block):
    rest = block.shape[4:]
    shaped = block.reshape((NKX, NKY // 2, KZB, 2, 2) + rest)
    shaped = jnp.take(shaped, brick_order(), axis=2)
    shaped = jnp.moveaxis(shaped, 3, 2)
    return shaped.reshape((NKX, NKY, NKZ) + rest)


def from_grid(block):
    rest = block.shape[3:]
    shaped = block.reshape((NKX, NKY // 2, 2, KZB, 2) + rest)
    shaped = jnp.moveaxis(shaped, 2, 3)
    shaped = jnp.take(shaped, brick_order(), axis=2)
    return shaped.reshape((NKX, (NKY // 2) * KZB, 2, 2) + rest)


def swap_last(block):
    return jnp.swapaxes(block, -1, -2)


def column_terms(q_re, q_im, e_re, e_im, charge):
    denom = e_re * e_re + e_im * e_im
    col_re = e_re[..., None, :]
    col_im = e_im[..., None, :]
    r_re = q_re * col_re + q_im * col_im
    r_im = q_im * col_re - q_re * col_im
    s_re = (charge * e_re / denom)[..., None, :]
    s_im = (-charge * e_im / denom)[..., None, :]
    t_re = q_re * s_re - q_im * s_im
    t_im = q_re * s_im + q_im * s_re
    out_re = 0.5 * (r_re - swap_last(r_re)) - 0.5 * (t_im - swap_last(t_im))
    out_im = 0.5 * (r_im + swap_last(r_im)) + 0.5 * (t_re + swap_last(t_re))
    return out_re, out_im


def plane_product(pieces):
    gauge, inner, beside = pieces
    x_re = jnp.einsum("yzij,yzjl->yzil", inner[:, :, 0], beside[:, :, 0], precision=highest) - jnp.einsum("yzij,yzjl->yzil", inner[:, :, 1], beside[:, :, 1], precision=highest)
    x_im = jnp.einsum("yzij,yzjl->yzil", inner[:, :, 0], beside[:, :, 1], precision=highest) + jnp.einsum("yzij,yzjl->yzil", inner[:, :, 1], beside[:, :, 0], precision=highest)
    p_re = jnp.einsum("yzji,yzjl->yzil", gauge[:, :, 0], x_re, precision=highest) + jnp.einsum("yzji,yzjl->yzil", gauge[:, :, 1], x_im, precision=highest)
    p_im = jnp.einsum("yzji,yzjl->yzil", gauge[:, :, 0], x_im, precision=highest) - jnp.einsum("yzji,yzjl->yzil", gauge[:, :, 1], x_re, precision=highest)
    return p_re, p_im


def reference(intersections, rotations, offsets, weights, basis):
    count_b = offsets.shape[0]
    u_grid = to_grid(rotations)
    m_grid = to_grid(intersections)
    step_vec = jnp.dot(offsets.astype(jnp.float32), basis, precision=highest)
    parts_re = []
    parts_im = []
    for index in range(count_b):
        moves = (-offsets[index, 0], -offsets[index, 1], -offsets[index, 2])
        beside = jnp.roll(u_grid, moves, axis=(0, 1, 2))
        made_re, made_im = lax.map(plane_product, (u_grid, m_grid[:, :, :, index], beside))
        parts_re.append(made_re)
        parts_im.append(made_im)
    p_re = jnp.stack(parts_re)
    p_im = jnp.stack(parts_im)
    d_re = jnp.diagonal(p_re, axis1=-2, axis2=-1)
    d_im = jnp.diagonal(p_im, axis1=-2, axis2=-1)
    phase = jnp.arctan2(d_im, d_re)
    cen_total = jnp.einsum("b,bc,bxyzn->cn", weights, step_vec, phase, precision=highest)
    spread_total = jnp.sum(weights[:, None, None, None, None] * (1.0 - d_re * d_re - d_im * d_im + phase * phase))
    centres = (-2.0 / NK) * cen_total
    spread = (2.0 / NK) * spread_total - jnp.sum(centres * centres)
    along = jnp.einsum("bc,cn->bn", step_vec, centres, precision=highest)
    grad = jnp.zeros((NKX, NKY, NKZ, 2) + p_re.shape[-2:], jnp.float32)
    for index in range(count_b):
        charge = phase[index] + along[index]
        fwd = column_terms(p_re[index], p_im[index], d_re[index], d_im[index], charge)
        adj = column_terms(swap_last(p_re[index]), -swap_last(p_im[index]), d_re[index], -d_im[index], -charge)
        moves = (offsets[index, 0], offsets[index, 1], offsets[index, 2])
        grad = grad + weights[index] * jnp.stack(fwd, 3)
        grad = grad + jnp.roll(weights[index] * jnp.stack(adj, 3), moves, axis=(0, 1, 2))
    return from_grid(4.0 * grad), centres, spread
```

```python
import jax
import jax.numpy as jnp
import numpy as np
from jax import lax
from jax.experimental import pallas as pl
from jax.experimental.pallas import tpu as pltpu
from jax.sharding import PartitionSpec as P

NB = 6
KZB = 4
J = 128
NKX = 8
NYZ = 32
NK = 1024
AXES = ("kx", "kyz")

highest = lax.Precision.HIGHEST

UNITS = [(1, 0, 0), (0, 1, 0), (0, 0, 1)]
DIAGONALS = [
    (1, 1, 0),
    (1, -1, 0),
    (1, 0, 1),
    (1, 0, -1),
    (0, 1, 1),
    (0, 1, -1),
    (1, 1, 1),
    (1, 1, -1),
    (1, -1, 1),
    (1, -1, -1),
]
FIXED = 12
GRAY = [0, 1, 3, 2]


def place(step, k):
    row, col = k // 2 + step[1], k % 2 + step[2]
    return (step[0], row // 2, col // 2), (row % 2) * 2 + col % 2


def beside_device(device, delta):
    x, r = device // NYZ, device % NYZ
    x = (x + delta[0]) % NKX
    y = (r // 4 + delta[1]) % (NYZ // 4)
    g = (GRAY[r % 4] + delta[2]) % KZB
    return x * NYZ + y * 4 + GRAY[g]


def route_from(delta):
    return [(beside_device(i, delta), i) for i in range(NKX * NYZ)]


def route_to(delta):
    return [(i, beside_device(i, delta)) for i in range(NKX * NYZ)]


def make_plan(step):
    known = {}
    for t in range(4):
        known[((0, 0, 0), t)] = t
        known[((1, 0, 0), t)] = 4 + t
    known[((0, 1, 0), 0)] = 8
    known[((0, 0, 1), 0)] = 9
    known[((0, 0, 1), 2)] = 10
    fetched, sent = {}, {}
    for k in range(4):
        where = place(step, k)
        if where in known:
            continue
        delta, t = where
        if delta[1] != 0 and k % 2 == 1:
            sent.setdefault(delta, []).append(k)
        else:
            fetched.setdefault(delta, []).append(t)
    groups, slots_u, slots_v, target = [], {}, {}, []
    for delta in sorted(fetched):
        groups.append(("u", delta, len(target), fetched[delta]))
        for t in fetched[delta]:
            slots_u[(delta, t)] = len(target)
            target.append(t)
    for delta in sorted(sent):
        groups.append(("v", delta, len(target), sent[delta]))
        for k in sent[delta]:
            slots_v[k] = len(target)
            target.append(k)
    pairs = []
    for k in range(4):
        delta, t = place(step, k)
        if k in slots_v:
            pairs.append((("got", slots_v[k]), t, ("got", slots_v[k]), t))
        elif (delta, t) in known:
            at = known[(delta, t)]
            pairs.append((("own", k), at, k, at))
        else:
            at = ("got", slots_u[(delta, t)])
            pairs.append((("own", k), at, k, at))
    return groups, target, pairs


PLANS = [make_plan(step) for step in DIAGONALS]
EXTRA = max(len(plan[1]) for plan in PLANS)
RIGHTS = 11 + 3 * EXTRA
SLOTS = FIXED + 3 * EXTRA
WIDTH = 17 + EXTRA


def table_row(which, plan):
    def at(value, own, got):
        if isinstance(value, tuple):
            return value[1] + (own if value[0] == "own" else got)
        return value

    groups, target, pairs = plan
    first = which * EXTRA
    row = [at(p[0], 0, 4) for p in pairs] + [at(p[1], 0, 11 + first) for p in pairs]
    row += [at(p[2], 0, FIXED + first) for p in pairs] + [at(p[3], 0, FIXED + first) for p in pairs]
    return row + target + [0] * (EXTRA - len(target)) + [len(target)]


TABLE = np.array([[table_row(j, plan) for plan in PLANS] for j in range(3)], np.int32)


def unit_pair(j, k):
    delta, t = place(UNITS[j], k)
    if (j, k) == (1, 3):
        return t, 11, t
    if delta == (0, 0, 0):
        return t, k, t
    at = {0: 4 + t, 1: 8, 2: 9 + t // 2}[j]
    return at, k, at


CODES = np.array([(s[0] + 1) * 9 + (s[1] + 1) * 3 + s[2] + 1 for s in UNITS + DIAGONALS], np.int32)


def halves(x):
    hi = x.astype(jnp.bfloat16)
    return hi, (x - hi.astype(jnp.float32)).astype(jnp.bfloat16)


def three(a_hi, a_lo, b_hi, b_lo):
    def dot(a, b):
        return lax.dot_general(a, b, (((1,), (0,)), ((), ())), preferred_element_type=jnp.float32)

    return dot(a_hi, b_hi) + (dot(a_hi, b_lo) + dot(a_lo, b_hi))


VMEM = pl.BlockSpec(memory_space=pltpu.VMEM)
SMEM = pl.BlockSpec(memory_space=pltpu.SMEM)
PARAMS = pltpu.CompilerParams(vmem_limit_bytes=48 * 1024 * 1024)


def mats(n):
    return jax.ShapeDtypeStruct((n, 2, J, J), jnp.float32)


def reals(n):
    return jax.ShapeDtypeStruct((n, J, J), jnp.float32)


def left_kernel(rows, u_ref, m_ref, v_ref, vy_ref, b_hi, b_lo):
    k = pl.program_id(0)
    a_hi, a_lo = halves(jnp.concatenate([u_ref[0, 0].T, u_ref[0, 1].T], 1))

    for j in range(NB):
        row = rows[j]
        re, im = halves(m_ref[0, row, 0]), halves(m_ref[0, row, 1])
        for ref, which in ((b_hi, 0), (b_lo, 1)):
            ref[j % 2, :J, :J] = re[which]
            ref[j % 2, :J, J:] = im[which]
            ref[j % 2, J:, :J] = im[which]
            ref[j % 2, J:, J:] = -re[which]
        made = three(a_hi, a_lo, b_hi[j % 2], b_lo[j % 2])
        v_ref[j, 0, 0] = made[:, :J]
        v_ref[j, 0, 1] = made[:, J:]
        if j == 1:
            vy_ref[0, 0] = made[:, :J]
            vy_ref[0, 1] = made[:, J:]


def left_products(rows, own_u, local_m):
    return pl.pallas_call(
        left_kernel,
        grid_spec=pltpu.PrefetchScalarGridSpec(
            num_scalar_prefetch=1,
            grid=(4,),
            in_specs=[
                pl.BlockSpec((1, 2, J, J), lambda k, rows: (k, 0, 0, 0)),
                pl.BlockSpec((1, NB, 2, J, J), lambda k, rows: (k, 0, 0, 0, 0)),
            ],
            out_specs=[
                pl.BlockSpec((NB, 1, 2, J, J), lambda k, rows: (0, k, 0, 0, 0)),
                pl.BlockSpec((1, 2, J, J), lambda k, rows: (0, 0, 0, 0)),
            ],
            scratch_shapes=[
                pltpu.VMEM((2, 2 * J, 2 * J), jnp.bfloat16),
                pltpu.VMEM((2, 2 * J, 2 * J), jnp.bfloat16),
            ],
        ),
        out_shape=[jax.ShapeDtypeStruct((NB, 4, 2, J, J), jnp.float32), mats(1)],
        compiler_params=PARAMS,
        cost_estimate=pl.CostEstimate(flops=1 << 30, bytes_accessed=8 << 20, transcendentals=0),
        name="left_products",
    )(rows, own_u, local_m)


def pair_kernel(tab, u_ref, ux_ref, uy_ref, uz_ref, vy_ref, e0_ref, e1_ref, e2_ref, v_ref, p_ref, d_ref, b_hi, b_lo):
    extra = (e0_ref, e1_ref, e2_ref)

    def block(at, re, im):
        for ref, part_re, part_im in zip((b_hi, b_lo), halves(re), halves(im)):
            ref[at, :J, :J] = part_re
            ref[at, :J, J:] = part_im
            ref[at, J:, :J] = -part_im
            ref[at, J:, J:] = part_re

    at = 0
    for ref, n in ((u_ref, 4), (ux_ref, 4), (uy_ref, 1), (uz_ref, 2)) + tuple((e, EXTRA) for e in extra):
        for i in range(n):
            block(at, ref[i, 0], ref[i, 1])
            at += 1
    eye = lax.broadcasted_iota(jnp.int32, (J, J), 0) == lax.broadcasted_iota(jnp.int32, (J, J), 1)

    def pair(p, right, re, im):
        a_hi, a_lo = halves(jnp.concatenate([re, im], 1))
        made = three(a_hi, a_lo, b_hi[right], b_lo[right])
        p_ref[p, 0] = made[:, :J]
        p_ref[p, 1] = made[:, J:]
        d_ref[0, p : p + 1, :] = jnp.sum(jnp.where(eye, made[:, :J], 0.0), 0, keepdims=True)
        d_ref[1, p : p + 1, :] = jnp.sum(jnp.where(eye, made[:, J:], 0.0), 0, keepdims=True)

    for p in range(24):
        j, k = p // 4, p % 4
        if p == 7:
            pair(p, unit_pair(1, 3)[0], vy_ref[0, 0], vy_ref[0, 1])
        elif p < 12:
            pair(p, unit_pair(j, k)[0], v_ref[p, 0], v_ref[p, 1])
        else:
            left = tab[j - 3, k]
            mine = 4 * j + jnp.minimum(left, 3)
            got = jnp.maximum(left - 4, 0)
            re = jnp.where(left < 4, v_ref[mine, 0], extra[j - 3][got, 0])
            im = jnp.where(left < 4, v_ref[mine, 1], extra[j - 3][got, 1])
            pair(p, tab[j - 3, 4 + k], re, im)


def pair_products(tab, own_u, ux, uy, uz, vy, more, v):
    return pl.pallas_call(
        pair_kernel,
        in_specs=[SMEM] + [VMEM] * 9,
        out_specs=[VMEM, VMEM],
        out_shape=[mats(24), jax.ShapeDtypeStruct((2, 24, J), jnp.float32)],
        scratch_shapes=[
            pltpu.VMEM((RIGHTS, 2 * J, 2 * J), jnp.bfloat16),
            pltpu.VMEM((RIGHTS, 2 * J, 2 * J), jnp.bfloat16),
        ],
        compiler_params=PARAMS,
        cost_estimate=pl.CostEstimate(flops=1 << 30, bytes_accessed=8 << 20, transcendentals=0),
        name="pair_products",
    )(tab, own_u, ux, uy, uz, vy, *more, v)


def term_kernel(tab, p_ref, coef_ref, turned_ref, own_ref, x_ref, y_ref, z_ref, vy_ref, e0_ref, e1_ref, e2_ref, plain, cross):
    plain[...] = jnp.zeros_like(plain)
    cross[...] = jnp.zeros_like(cross)
    for p in range(24):
        j, k = p // 4, p % 4
        if j < 3:
            _, low, up = unit_pair(j, k)
        else:
            low, up = tab[j - 3, 8 + k], tab[j - 3, 12 + k]
        re, im = p_ref[p, 0], p_ref[p, 1]
        a, b = coef_ref[0, p : p + 1, :], coef_ref[1, p : p + 1, :]
        plain[low] += re * a + im * b
        cross[low] += im * a - re * b
        a, b = turned_ref[0, :, p : p + 1], turned_ref[1, :, p : p + 1]
        plain[up] -= re * a + im * b
        cross[up] += re * b - im * a
    at = 0
    outs = ((own_ref, 4), (x_ref, 4), (y_ref, 1), (z_ref, 2), (vy_ref, 1))
    for ref, n in outs + ((e0_ref, EXTRA), (e1_ref, EXTRA), (e2_ref, EXTRA)):
        for i in range(n):
            ref[i] = 2.0 * (plain[at] + cross[at].T)
            at += 1


def pair_terms(tab, p, coef, turned):
    return pl.pallas_call(
        term_kernel,
        in_specs=[SMEM] + [VMEM] * 3,
        out_specs=[VMEM] * 8,
        out_shape=[reals(4), reals(4), reals(1), reals(2), reals(1)] + [reals(EXTRA)] * 3,
        scratch_shapes=[pltpu.VMEM((SLOTS, J, J), jnp.float32), pltpu.VMEM((SLOTS, J, J), jnp.float32)],
        compiler_params=PARAMS,
        cost_estimate=pl.CostEstimate(flops=1 << 24, bytes_accessed=8 << 20, transcendentals=0),
        name="pair_terms",
    )(tab, p, coef, turned)


def fold_kernel(tab, own_ref, x_ref, y_ref, z_ref, vy_ref, e0_ref, e1_ref, e2_ref, g_ref, total):
    for k in range(4):
        total[k] = own_ref[k] + x_ref[k]
    total[0] += y_ref[0] + z_ref[0]
    total[2] += z_ref[1]
    total[3] += vy_ref[0]
    for j, ref in enumerate((e0_ref, e1_ref, e2_ref)):
        for i in range(EXTRA):

            @pl.when(i < tab[j, 16 + EXTRA])
            def _():
                total[tab[j, 16 + i]] += ref[i]

    for k in range(4):
        turned = total[k].T
        g_ref[k, 0] = 0.5 * (total[k] - turned)
        g_ref[k, 1] = 0.5 * (total[k] + turned)


def fold_terms(tab, own, x, y, z, vy, more):
    return pl.pallas_call(
        fold_kernel,
        in_specs=[SMEM] + [VMEM] * 8,
        out_specs=VMEM,
        out_shape=mats(4),
        scratch_shapes=[pltpu.VMEM((4, J, J), jnp.float32)],
        compiler_params=PARAMS,
        name="fold_terms",
    )(tab, own, x, y, z, vy, *more)


def move(block, route):
    return lax.ppermute(block, AXES, route)


def padded(parts, used, shape):
    if used < EXTRA:
        parts = parts + [jnp.zeros((EXTRA - used,) + shape, jnp.float32)]
    return jnp.concatenate(parts, 0)


def fetch_branch(plan, j):
    def branch(own_u, v):
        parts = []
        for kind, delta, _, members in plan[0]:
            if kind == "u":
                block = jnp.concatenate([own_u[t : t + 1] for t in members], 0)
                parts.append(move(block, route_from(delta)))
            else:
                block = jnp.concatenate([v[j, k][None] for k in members], 0)
                parts.append(move(block, route_to(delta)))
        return padded(parts, len(plan[1]), (2, J, J))

    return branch


def return_branch(plan):
    def branch(more):
        parts = []
        for kind, delta, start, members in plan[0]:
            block = more[start : start + len(members)]
            route = route_to(delta) if kind == "u" else route_from(delta)
            parts.append(move(block, route))
        return padded(parts, len(plan[1]), (J, J))

    return branch


def over_all(x):
    def stage(x, axis, count, shifts):
        got = [
            lax.ppermute(x, axis, [(i, i ^ s) for i in range(count)]) for s in shifts
        ]
        if len(got) == 1:
            return x + got[0]
        return (x + got[0]) + (got[1] + got[2])

    x = stage(x, "kyz", NYZ, (1,))
    x = stage(x, "kx", NKX, (1,))
    x = stage(x, "kx", NKX, (2, 4, 6))
    x = stage(x, "kyz", NYZ, (2, 4, 6))
    return stage(x, "kyz", NYZ, (8, 16, 24))


def fast(present, row_of, intersections, rotations, offsets, weights, basis):
    own_u = rotations.reshape(4, 2, J, J)
    local_m = intersections.reshape(4, NB, 2, J, J)
    ux = move(own_u, route_from((1, 0, 0)))
    uy = move(own_u[0:1], route_from((0, 1, 0)))
    uz = move(own_u[0::2], route_from((0, 0, 1)))

    rank = jnp.cumsum(present[3:].astype(jnp.int32))
    nth = (rank[None, :] == jnp.arange(1, 4, dtype=jnp.int32)[:, None]) & present[None, 3:]
    rows = jnp.concatenate([row_of[:3], jnp.sum(jnp.where(nth, row_of[None, 3:], 0), 1)])
    kind = jnp.sum(jnp.where(nth, jnp.arange(10, dtype=jnp.int32)[None, :], 0), 1)
    tab = jnp.sum(jnp.where(nth[:, :, None], jnp.asarray(TABLE), 0), 1)

    v, vy_out = left_products(rows, own_u, local_m)
    vy = move(vy_out, route_to((0, 1, 0)))
    more = [
        lax.switch(kind[j] - j, [fetch_branch(plan, 3 + j) for plan in PLANS[j : j + 8]], own_u, v)
        for j in range(3)
    ]
    p, d = pair_products(tab, own_u, ux, uy, uz, vy, more, v.reshape(24, 2, J, J))

    d_re, d_im = d[0].reshape(NB, 4, J), d[1].reshape(NB, 4, J)
    phase = jnp.arctan2(d_im, d_re)
    step_vec = jnp.sum(offsets.astype(jnp.float32)[:, :, None] * basis[None], 1)
    pick = rows[:, None] == jnp.arange(NB, dtype=jnp.int32)[None, :]
    scale = jnp.sum(jnp.where(pick, weights[None, :], 0.0), 1)
    step_vec = jnp.sum(jnp.where(pick[:, :, None], step_vec[None], 0.0), 1)
    cen_part = jnp.sum((scale[:, None] * step_vec)[:, :, None] * jnp.sum(phase, 1)[:, None, :], 0)
    norm = d_re * d_re + d_im * d_im
    spread_part = jnp.sum(scale[:, None, None] * (1.0 - norm + phase * phase), (0, 1))
    total = over_all(jnp.concatenate([cen_part, spread_part[None]], 0))
    centres = (-2.0 / NK) * total[:3]
    spread = (2.0 / NK) * jnp.sum(total[3]) - jnp.sum(centres * centres)
    along = jnp.sum(step_vec[:, :, None] * centres[None], 1)
    charge = phase + along[:, None]
    f_re = scale[:, None, None] * (d_re + charge * d_im / norm)
    f_im = scale[:, None, None] * (charge * d_re / norm - d_im)
    coef = jnp.stack([f_re + f_im, f_re - f_im]).reshape(2, 24, J)
    own, gx, gy, gz, gvy, *gmore = pair_terms(tab, p, coef, jnp.swapaxes(coef, 1, 2))

    gx = move(gx, route_to((1, 0, 0)))
    gy = move(gy, route_to((0, 1, 0)))
    gz = move(gz, route_to((0, 0, 1)))
    gvy = move(gvy, route_from((0, 1, 0)))
    gmore = [
        lax.switch(kind[j] - j, [return_branch(plan) for plan in PLANS[j : j + 8]], gmore[j])
        for j in range(3)
    ]
    gradient = fold_terms(tab, own, gx, gy, gz, gvy, gmore)
    return gradient.reshape(1, 1, 2, 2, 2, J, J), centres, spread


def shifted(block, axis, distance):
    devices = range(lax.axis_size(axis))
    route = [((i - distance) % len(devices), i) for i in devices]
    return lax.ppermute(block, axis, route)


def from_partner(block, axis, stride):
    count = lax.axis_size(axis)
    route = []
    for low in range(count):
        high = low | 1 << stride
        if high != low and high < count:
            route += [(low, high), (high, low)]
    return lax.ppermute(block, axis, route)


def from_brick(block, steps):
    return shifted(block, "kyz", steps)


def from_pair(block, which):
    return from_partner(block, "kyz", which)


def from_plane(block, steps):
    return shifted(block, "kx", steps)


def back_brick(block, steps):
    return shifted(block, "kyz", steps)


def back_pair(block, which):
    return from_partner(block, "kyz", which)


def back_plane(block, steps):
    return shifted(block, "kx", steps)


def centre_totals(cen_part, spread_part):
    return lax.psum((cen_part, spread_part), ("kx", "kyz"))


def widen_kx(block):
    return jnp.concatenate([from_plane(block, 1), block, from_plane(block, -1)], 0)


def widen_ky(block):
    return jnp.concatenate(
        [from_brick(block[:, -1:], KZB), block, from_brick(block[:, :1], -KZB)], 1
    )


def widen_kz(block, upward):
    first_face = block[:, :, :1]
    last_face = block[:, :, -1:]
    got_zero = from_pair(jnp.where(upward, last_face, first_face), 0)
    got_one = from_pair(jnp.where(upward, first_face, last_face), 1)
    left_side = jnp.where(upward, got_one, got_zero)
    right_side = jnp.where(upward, got_zero, got_one)
    return jnp.concatenate([left_side, block, right_side], 2)


def fold_kx(block):
    return block[1:2] + back_plane(block[2:3], 1) + back_plane(block[0:1], -1)


def fold_ky(block):
    into_low = back_brick(block[:, 3:4], KZB)
    into_high = back_brick(block[:, 0:1], -KZB)
    return jnp.concatenate([block[:, 1:2] + into_low, block[:, 2:3] + into_high], 1)


def fold_kz(block, upward):
    low_rim = block[:, :, 0:1]
    high_rim = block[:, :, 3:4]
    got_zero = back_pair(jnp.where(upward, high_rim, low_rim), 0)
    got_one = back_pair(jnp.where(upward, low_rim, high_rim), 1)
    into_low = jnp.where(upward, got_one, got_zero)
    into_high = jnp.where(upward, got_zero, got_one)
    return jnp.concatenate([block[:, :, 1:2] + into_low, block[:, :, 2:3] + into_high], 2)


def swap_last(block):
    return jnp.swapaxes(block, -1, -2)


def column_terms(q_re, q_im, e_re, e_im, charge):
    denom = e_re * e_re + e_im * e_im
    col_re = e_re[..., None, :]
    col_im = e_im[..., None, :]
    r_re = q_re * col_re + q_im * col_im
    r_im = q_im * col_re - q_re * col_im
    s_re = (charge * e_re / denom)[..., None, :]
    s_im = (-charge * e_im / denom)[..., None, :]
    t_re = q_re * s_re - q_im * s_im
    t_im = q_re * s_im + q_im * s_re
    out_re = 0.5 * (r_re - swap_last(r_re)) - 0.5 * (t_im - swap_last(t_im))
    out_im = 0.5 * (r_im + swap_last(r_im)) + 0.5 * (t_re + swap_last(t_re))
    return (out_re, out_im)


def slow(intersections, rotations, offsets, weights, basis):
    width = rotations.shape[-1]
    own_u = rotations.reshape(4, 2, width, width)
    local_m = intersections.reshape(4, NB, 2, width, width)
    position = lax.axis_index("kyz") % KZB
    upward = jnp.logical_or(position == 0, position == 3)
    start = rotations.reshape(1, 2, 2, 2, width, width)
    widened = widen_ky(widen_kz(widen_kx(start), upward))
    flat_u = widened.reshape(48, 2, width, width)
    local_k = jnp.arange(4, dtype=jnp.int32)
    row_a = local_k // 2
    col_c = local_k % 2
    beside_slot = (
        (1 + offsets[None, :, 0]) * 16
        + (1 + row_a[:, None] + offsets[None, :, 1]) * 4
        + (1 + col_c[:, None] + offsets[None, :, 2])
    )
    own_slot = jnp.broadcast_to((16 + (1 + row_a) * 4 + 1 + col_c)[:, None], (4, NB))
    beside = jnp.take(flat_u, beside_slot.reshape(-1), axis=0).reshape(4, NB, 2, width, width)
    x_re = jnp.einsum(
        "kbij,kbjl->kbil", local_m[:, :, 0], beside[:, :, 0], precision=highest
    ) - jnp.einsum("kbij,kbjl->kbil", local_m[:, :, 1], beside[:, :, 1], precision=highest)
    x_im = jnp.einsum(
        "kbij,kbjl->kbil", local_m[:, :, 0], beside[:, :, 1], precision=highest
    ) + jnp.einsum("kbij,kbjl->kbil", local_m[:, :, 1], beside[:, :, 0], precision=highest)
    p_re = jnp.einsum("kji,kbjl->kbil", own_u[:, 0], x_re, precision=highest) + jnp.einsum(
        "kji,kbjl->kbil", own_u[:, 1], x_im, precision=highest
    )
    p_im = jnp.einsum("kji,kbjl->kbil", own_u[:, 0], x_im, precision=highest) - jnp.einsum(
        "kji,kbjl->kbil", own_u[:, 1], x_re, precision=highest
    )
    d_re = jnp.diagonal(p_re, axis1=-2, axis2=-1)
    d_im = jnp.diagonal(p_im, axis1=-2, axis2=-1)
    phase = jnp.arctan2(d_im, d_re)
    step_vec = jnp.dot(offsets.astype(jnp.float32), basis, precision=highest)
    cen_part = jnp.einsum("b,bc,kbn->cn", weights, step_vec, phase, precision=highest)
    spread_part = jnp.sum(
        weights[None, :, None] * (1.0 - d_re * d_re - d_im * d_im + phase * phase)
    )
    count = lax.axis_size("kx") * lax.axis_size("kyz") * 4
    a_re = swap_last(p_re)
    a_im = -swap_last(p_im)
    slots = jnp.concatenate([own_slot, beside_slot], 0).reshape(-1)
    selector = (slots[:, None] == jnp.arange(48, dtype=jnp.int32)[None, :]).astype(jnp.float32)
    scaled_w = weights[None, :, None, None, None]
    cen_total, spread_total = centre_totals(cen_part, spread_part)
    centres = -2.0 / count * cen_total
    along = jnp.einsum("bc,cn->bn", step_vec, centres, precision=highest)
    charge = phase + along[None]
    fwd = column_terms(p_re, p_im, d_re, d_im, charge)
    adj = column_terms(a_re, a_im, d_re, -d_im, -charge)
    contrib = jnp.concatenate([jnp.stack(fwd, 2), jnp.stack(adj, 2)], 0) * scaled_w
    gathered = jnp.dot(selector.T, contrib.reshape(48, -1), precision=highest).reshape(
        48, 2, width, width
    )
    spread = 2.0 / count * spread_total - jnp.sum(centres * centres)
    grid = gathered.reshape(3, 4, 4, 2, width, width)
    folded = fold_kx(fold_kz(fold_ky(grid), upward))
    gradient = (4.0 * folded).reshape(1, 1, 2, 2, 2, width, width)
    return (gradient, centres, spread)


def on_device(intersections, rotations, offsets, weights, basis):
    code = (offsets[:, 0] + 1) * 9 + (offsets[:, 1] + 1) * 3 + offsets[:, 2] + 1
    same = jnp.asarray(CODES)[:, None] == code[None, :]
    present = jnp.any(same, 1)
    row_of = jnp.sum(jnp.where(same, jnp.arange(NB, dtype=jnp.int32)[None, :], 0), 1)
    operands = (intersections, rotations, offsets, weights, basis)
    return lax.cond(
        jnp.sum(present.astype(jnp.int32)) == NB,
        lambda *args: fast(present, row_of, *args),
        slow,
        *operands,
    )


def solution(mesh):
    placed = (
        P("kx", "kyz", None, None, None, None, None, None),
        P("kx", "kyz", None, None, None, None, None),
        P(),
        P(),
        P(),
    )
    return jax.shard_map(
        on_device,
        mesh=mesh,
        in_specs=placed,
        out_specs=(P("kx", "kyz", None, None, None, None, None), P(), P()),
        check_vma=False,
    )
```

```python
import functools

import jax
import jax.numpy as jnp
import numpy as np
from jax import lax
from jax.experimental import pallas as pl
from jax.experimental.pallas import tpu as pltpu
from jax.sharding import PartitionSpec as P

NB = 6
KZB = 4
J = 128
NKX = 8
NYZ = 32
NK = 1024
AXES = ("kx", "kyz")

UNITS = [(1, 0, 0), (0, 1, 0), (0, 0, 1)]
DIAGONALS = [
    (1, 1, 0),
    (1, -1, 0),
    (1, 0, 1),
    (1, 0, -1),
    (0, 1, 1),
    (0, 1, -1),
    (1, 1, 1),
    (1, 1, -1),
    (1, -1, 1),
    (1, -1, -1),
]
GRAY = [0, 1, 3, 2]
GROUPS = (
    [((0, 0, 0), t) for t in range(4)],
    [((1, 0, 0), t) for t in range(4)],
    [((0, 1, 0), 0), ((0, 1, 0), 1)],
    [((1, 1, 0), 0), ((1, 1, 0), 1)],
    [((1, -1, 0), 2), ((1, -1, 0), 3)],
    [((0, 0, 1), 0), ((0, 0, 1), 2), ((0, 1, 1), 0), ((1, 0, 1), 0), ((1, 0, 1), 2)],
    [((0, 0, -1), 3), ((0, 1, -1), 1), ((1, 0, -1), 1), ((1, 0, -1), 3)],
    [((1, 1, 1), 0), ((1, -1, 1), 2)],
    [((1, 1, -1), 1), ((1, -1, -1), 3)],
)
SIZES = [len(group) for group in GROUPS]
SLOTS = sum(SIZES)
SLOT_OF = {where: i for i, where in enumerate(sum(GROUPS, []))}


def place(step, k):
    row, col = k // 2 + step[1], k % 2 + step[2]
    return (step[0], row // 2, col // 2), (row % 2) * 2 + col % 2


def beside_device(device, delta):
    x, r = device // NYZ, device % NYZ
    x = (x + delta[0]) % NKX
    y = (r // 4 + delta[1]) % (NYZ // 4)
    g = (GRAY[r % 4] + delta[2]) % KZB
    return x * NYZ + y * 4 + GRAY[g]


def upper_slots(step):
    return [SLOT_OF[place(step, k)] for k in range(4)]


UNIT_SLOTS = [upper_slots(step) for step in UNITS]
TABLE = np.array([upper_slots(step) for step in DIAGONALS], np.int32)
CODES = np.array([(s[0] + 1) * 9 + (s[1] + 1) * 3 + s[2] + 1 for s in UNITS + DIAGONALS], np.int32)


def halves(x):
    hi = x.astype(jnp.bfloat16)
    return hi, (x - hi.astype(jnp.float32)).astype(jnp.bfloat16)


def three(a_hi, a_lo, b_hi, b_lo):
    def dot(a, b):
        return lax.dot_general(a, b, (((1,), (0,)), ((), ())), preferred_element_type=jnp.float32)

    return dot(a_hi, b_hi) + (dot(a_hi, b_lo) + dot(a_lo, b_hi))


VMEM = pl.BlockSpec(memory_space=pltpu.VMEM)
SMEM = pl.BlockSpec(memory_space=pltpu.SMEM)
PARAMS = pltpu.CompilerParams(vmem_limit_bytes=48 * 1024 * 1024)


def mats(n):
    return jax.ShapeDtypeStruct((n, 2, J, J), jnp.float32)


def reals(n):
    return jax.ShapeDtypeStruct((n, J, J), jnp.float32)


def block(ref_hi, ref_lo, at, re, im, sign):
    for ref, part_re, part_im in zip((ref_hi, ref_lo), halves(re), halves(im)):
        ref[at, :J, :J] = part_re
        ref[at, :J, J:] = part_im
        ref[at, J:, :J] = -part_im if sign > 0 else part_im
        ref[at, J:, J:] = part_re if sign > 0 else -part_re


def left_kernel(u_ref, m_ref, v_ref, b_hi, b_lo):
    a_hi, a_lo = halves(jnp.concatenate([u_ref[0, 0].T, u_ref[0, 1].T], 1))
    for j in range(NB):
        block(b_hi, b_lo, j % 2, m_ref[0, j, 0], m_ref[0, j, 1], -1)
        made = three(a_hi, a_lo, b_hi[j % 2], b_lo[j % 2])
        v_ref[0, j, 0] = made[:, :J]
        v_ref[0, j, 1] = made[:, J:]


def left_products(own_u, local_m):
    return pl.pallas_call(
        left_kernel,
        grid=(4,),
        in_specs=[
            pl.BlockSpec((1, 2, J, J), lambda k: (k, 0, 0, 0)),
            pl.BlockSpec((1, NB, 2, J, J), lambda k: (k, 0, 0, 0, 0)),
        ],
        out_specs=pl.BlockSpec((1, NB, 2, J, J), lambda k: (k, 0, 0, 0, 0)),
        scratch_shapes=[
            pltpu.VMEM((2, 2 * J, 2 * J), jnp.bfloat16),
            pltpu.VMEM((2, 2 * J, 2 * J), jnp.bfloat16),
        ],
        out_shape=jax.ShapeDtypeStruct((4, NB, 2, J, J), jnp.float32),
        compiler_params=PARAMS,
        cost_estimate=pl.CostEstimate(flops=1 << 32, bytes_accessed=8 << 20, transcendentals=0),
        name="left_products",
    )(own_u, local_m)


def pair_kernel(ends, rows, *refs, any_sign):
    parts, rest = refs[: len(SIZES)], refs[len(SIZES) :]
    if any_sign:
        v_ref, far_ref, p_ref, d_ref, slots, b_hi, b_lo = rest
    else:
        v_ref, p_ref, d_ref, slots, b_hi, b_lo = rest
    at = 0
    for ref, n in zip(parts, SIZES):
        slots[at : at + n] = ref[...]
        at += n
    eye = lax.broadcasted_iota(jnp.int32, (J, J), 0) == lax.broadcasted_iota(jnp.int32, (J, J), 1)
    for p in range(24):
        j, k = p // 4, p % 4
        if j < 3:
            low, up = k, UNIT_SLOTS[j][k]
        else:
            low, up = ends[0, j - 3, k], ends[1, j - 3, k]
        if any_sign and j >= 3:
            left = jnp.concatenate([far_ref[j - 3, low, 0], far_ref[j - 3, low, 1]], 1)
        else:
            row = rows[j]
            left = jnp.concatenate([v_ref[k, row, 0], v_ref[k, row, 1]], 1)
        a_hi, a_lo = halves(left)
        at = p % 2
        block(b_hi, b_lo, at, slots[up, 0], slots[up, 1], 1)
        made = three(a_hi, a_lo, b_hi[at], b_lo[at])
        p_ref[p, 0] = made[:, :J]
        p_ref[p, 1] = made[:, J:]
        d_ref[0, j, k : k + 1, :] = jnp.sum(jnp.where(eye, made[:, :J], 0.0), 0, keepdims=True)
        d_ref[1, j, k : k + 1, :] = jnp.sum(jnp.where(eye, made[:, J:], 0.0), 0, keepdims=True)


def pair_products(ends, rows, parts, v, far=None):
    more = () if far is None else (far,)
    return pl.pallas_call(
        functools.partial(pair_kernel, any_sign=far is not None),
        in_specs=[SMEM, SMEM] + [VMEM] * (len(SIZES) + 1 + len(more)),
        out_specs=[VMEM, VMEM],
        out_shape=[mats(24), jax.ShapeDtypeStruct((2, NB, 4, J), jnp.float32)],
        scratch_shapes=[
            pltpu.VMEM((SLOTS, 2, J, J), jnp.float32),
            pltpu.VMEM((2, 2 * J, 2 * J), jnp.bfloat16),
            pltpu.VMEM((2, 2 * J, 2 * J), jnp.bfloat16),
        ],
        compiler_params=PARAMS,
        cost_estimate=pl.CostEstimate(flops=1 << 32, bytes_accessed=8 << 20, transcendentals=0),
        name="pair_products",
    )(ends, rows, *parts, v, *more)


def term_kernel(ends, row_data, p_ref, d_ref, phase_ref, got_ref, *refs):
    total_ref, outs = refs[0], refs[1 : 1 + len(SIZES)]
    plain, cross, rows_a, rows_b = refs[1 + len(SIZES) :]
    plain[...] = jnp.zeros_like(plain)
    cross[...] = jnp.zeros_like(cross)
    total = jnp.sum(got_ref[...], 0)
    total_ref[...] = total
    centres = (-2.0 / NK) * total[:3]
    for j in range(NB):
        along = centres[0:1] * row_data[j, 1]
        for c in range(1, 3):
            along += centres[c : c + 1] * row_data[j, 1 + c]
        d_re, d_im = d_ref[0, j], d_ref[1, j]
        ratio = (phase_ref[j] + along) / (d_re * d_re + d_im * d_im)
        f_re = row_data[j, 0] * (d_re + ratio * d_im)
        f_im = row_data[j, 0] * (ratio * d_re - d_im)
        rows_a[4 * j : 4 * j + 4, :] = f_re + f_im
        rows_b[4 * j : 4 * j + 4, :] = f_re - f_im
    turned_a, turned_b = rows_a[...].T, rows_b[...].T
    for p in range(24):
        j, k = p // 4, p % 4
        if j < 3:
            low, up = k, UNIT_SLOTS[j][k]
        else:
            low, up = ends[0, j - 3, k], ends[1, j - 3, k]
        re, im = p_ref[p, 0], p_ref[p, 1]
        a, b = rows_a[p : p + 1, :], rows_b[p : p + 1, :]
        plain[low] += re * a + im * b
        cross[low] += im * a - re * b
        a, b = turned_a[:, p : p + 1], turned_b[:, p : p + 1]
        plain[up] -= re * a + im * b
        cross[up] += re * b - im * a
    at = 0
    for ref, n in zip(outs, SIZES):
        for i in range(n):
            ref[i] = 2.0 * (plain[at] + cross[at].T)
            at += 1


def pair_terms(ends, row_data, p, d, phase, got):
    return pl.pallas_call(
        term_kernel,
        in_specs=[SMEM, SMEM] + [VMEM] * 4,
        out_specs=[VMEM] * (1 + len(SIZES)),
        out_shape=[jax.ShapeDtypeStruct((4, J), jnp.float32)] + [reals(n) for n in SIZES],
        scratch_shapes=[
            pltpu.VMEM((SLOTS, J, J), jnp.float32),
            pltpu.VMEM((SLOTS, J, J), jnp.float32),
            pltpu.VMEM((J, J), jnp.float32),
            pltpu.VMEM((J, J), jnp.float32),
        ],
        compiler_params=PARAMS,
        cost_estimate=pl.CostEstimate(flops=1 << 24, bytes_accessed=8 << 20, transcendentals=0),
        name="pair_terms",
    )(ends, row_data, p, d, phase, got)


def fold_kernel(own_ref, x_ref, y_ref, g_ref):
    for k in range(4):
        total = own_ref[k] + x_ref[k]
        if k < 2:
            total += y_ref[k]
        turned = total.T
        g_ref[k, 0] = 0.5 * (total - turned)
        g_ref[k, 1] = 0.5 * (total + turned)


def fold_terms(own, x, y):
    return pl.pallas_call(
        fold_kernel,
        in_specs=[VMEM] * 3,
        out_specs=VMEM,
        out_shape=mats(4),
        compiler_params=PARAMS,
        name="fold_terms",
    )(own, x, y)


def fetch(delta, *blocks):
    route = [(beside_device(i, delta), i) for i in range(NKX * NYZ)]
    return lax.ppermute(jnp.concatenate(blocks, 0), AXES, route)


def give_back(delta, block):
    route = [(i, beside_device(i, delta)) for i in range(NKX * NYZ)]
    return lax.ppermute(block, AXES, route)


X, Y, Y_BACK, Z, Z_BACK = (1, 0, 0), (0, 1, 0), (0, -1, 0), (0, 0, 1), (0, 0, -1)


def halo(own):
    x = fetch(X, own)
    y = fetch(Y, own[0:2])
    xy = fetch(Y, x[0:2])
    xy_back = fetch(Y_BACK, x[2:4])
    z = fetch(Z, own[0::2], y[0:1], x[0::2])
    z_back = fetch(Z_BACK, own[3:4], y[1:2], x[1::2])
    corner = fetch(Z, xy[0:1], xy_back[0:1])
    corner_back = fetch(Z_BACK, xy[1:2], xy_back[1:2])
    return own, x, y, xy, xy_back, z, z_back, corner, corner_back


def fold_halo(own, x, y, xy, xy_back, z, z_back, corner, corner_back):
    corner = give_back(Z, corner)
    corner_back = give_back(Z_BACK, corner_back)
    z = give_back(Z, z)
    z_back = give_back(Z_BACK, z_back)
    xy = give_back(Y, xy + jnp.concatenate([corner[0:1], corner_back[0:1]], 0))
    xy_back = give_back(Y_BACK, xy_back + jnp.concatenate([corner[1:2], corner_back[1:2]], 0))
    y = give_back(Y, y + jnp.concatenate([z[2:3], z_back[1:2]], 0))
    beside = jnp.concatenate([z[3:4], z_back[2:3], z[4:5], z_back[3:4]], 0)
    x = give_back(X, x + beside + jnp.concatenate([xy, xy_back], 0))
    own = own + jnp.concatenate([z[0:1], jnp.zeros_like(z[0:1]), z[1:2], z_back[0:1]], 0)
    return fold_terms(own, x, y)


def over_all(x):
    return lax.all_to_all(jnp.broadcast_to(x[None], (NKX * NYZ,) + x.shape), AXES, 0, 0)


def on_device(intersections, rotations, offsets, weights, basis):
    own_u = rotations.reshape(4, 2, J, J)
    local_m = intersections.reshape(4, NB, 2, J, J)
    parts = halo(own_u)
    v = left_products(own_u, local_m)

    code = (offsets[:, 0] + 1) * 9 + (offsets[:, 1] + 1) * 3 + offsets[:, 2] + 1
    with_sign = jnp.asarray(CODES)[:, None] == code[None, :]
    against = 26 - jnp.asarray(CODES)[:, None] == code[None, :]
    here = with_sign | against
    rank = jnp.cumsum(jnp.any(here[3:], 1).astype(jnp.int32))
    nth = (rank[None] == jnp.arange(1, 4, dtype=jnp.int32)[:, None])[:, :, None] & here[None, 3:]
    chosen = jnp.concatenate([here[:3], jnp.any(nth, 1)], 0)
    rows = jnp.sum(jnp.where(chosen, jnp.arange(NB, dtype=jnp.int32)[None], 0), 1)
    upper = jnp.sum(jnp.where(jnp.any(nth, 2)[:, :, None], jnp.asarray(TABLE), 0), 1)
    lower = jnp.broadcast_to(jnp.arange(4, dtype=jnp.int32)[None], (3, 4))
    flipped = jnp.any(nth & against[None, 3:], (1, 2))
    ends = jnp.stack(
        [jnp.where(flipped[:, None], upper, lower), jnp.where(flipped[:, None], lower, upper)]
    )
    step_vec = jnp.sum(offsets.astype(jnp.float32)[:, :, None] * basis[None], 1)
    row_data = jnp.concatenate([weights[:, None], step_vec], 1)
    row_data = jnp.sum(jnp.where(chosen[:, :, None], row_data[None], 0.0), 1)

    def usual(ends, rows, v, *parts):
        return pair_products(ends, rows, parts, v)

    def any_sign(ends, rows, v, *parts):
        far = [jnp.concatenate(halo(v[:, rows[j]]), 0) for j in range(3, NB)]
        return pair_products(ends, rows, parts, v, jnp.stack(far))

    p, d = lax.cond(jnp.any(flipped), any_sign, usual, ends, rows, v, *parts)
    d_re, d_im = d[0], d[1]
    phase = jnp.arctan2(d_im, d_re)
    scale, step_vec = row_data[:, 0], row_data[:, 1:]
    cen_part = jnp.sum((scale[:, None] * step_vec)[:, :, None] * jnp.sum(phase, 1)[:, None, :], 0)
    norm = d_re * d_re + d_im * d_im
    spread_part = jnp.sum(scale[:, None, None] * (1.0 - norm + phase * phase), (0, 1))
    got = over_all(jnp.concatenate([cen_part, spread_part[None]], 0))
    total, *terms = pair_terms(ends, row_data, p, d, phase, got)
    gradient = fold_halo(*terms)
    centres = (-2.0 / NK) * total[:3]
    spread = (2.0 / NK) * jnp.sum(total[3]) - jnp.sum(centres * centres)
    return gradient.reshape(1, 1, 2, 2, 2, J, J), centres, spread


def solution(mesh):
    placed = (
        P("kx", "kyz", None, None, None, None, None, None),
        P("kx", "kyz", None, None, None, None, None),
        P(),
        P(),
        P(),
    )
    return jax.shard_map(
        on_device,
        mesh=mesh,
        in_specs=placed,
        out_specs=(P("kx", "kyz", None, None, None, None, None), P(), P()),
        check_vma=False,
    )
```

```python
import functools

import jax
import jax.numpy as jnp
import numpy as np
from jax import lax
from jax.experimental import pallas as pl
from jax.experimental.pallas import tpu as pltpu
from jax.sharding import PartitionSpec as P

NB = 6
KZB = 4
J = 128
NKX = 8
NYZ = 32
NK = 1024
AXES = ("kx", "kyz")

UNITS = [(1, 0, 0), (0, 1, 0), (0, 0, 1)]
DIAGONALS = [
    (1, 1, 0),
    (1, -1, 0),
    (1, 0, 1),
    (1, 0, -1),
    (0, 1, 1),
    (0, 1, -1),
    (1, 1, 1),
    (1, 1, -1),
    (1, -1, 1),
    (1, -1, -1),
]
GRAY = [0, 1, 3, 2]
GROUPS = (
    [((0, 0, 0), t) for t in range(4)],
    [((1, 0, 0), t) for t in range(4)],
    [((0, 1, 0), 0), ((0, 1, 0), 1)],
    [((1, 1, 0), 0), ((1, 1, 0), 1), ((1, -1, 0), 2), ((1, -1, 0), 3)],
    [((0, 0, 1), 0), ((0, 0, 1), 2)],
    [((0, 1, 1), 0), ((1, 0, 1), 0), ((1, 0, 1), 2)],
    [((0, 0, -1), 3)],
    [((0, 1, -1), 1), ((1, 0, -1), 1), ((1, 0, -1), 3)],
    [((1, 1, 1), 0), ((1, -1, 1), 2)],
    [((1, 1, -1), 1), ((1, -1, -1), 3)],
)
SIZES = [len(group) for group in GROUPS]
SLOTS = sum(SIZES)
BACK = SIZES[:4] + [SIZES[4] + SIZES[5], SIZES[6] + SIZES[7]] + SIZES[8:]
SLOT_OF = {where: i for i, where in enumerate(sum(GROUPS, []))}


def place(step, k):
    row, col = k // 2 + step[1], k % 2 + step[2]
    return (step[0], row // 2, col // 2), (row % 2) * 2 + col % 2


def beside_device(device, delta):
    x, r = device // NYZ, device % NYZ
    x = (x + delta[0]) % NKX
    y = (r // 4 + delta[1]) % (NYZ // 4)
    g = (GRAY[r % 4] + delta[2]) % KZB
    return x * NYZ + y * 4 + GRAY[g]


def upper_slots(step):
    return [SLOT_OF[place(step, k)] for k in range(4)]


UNIT_SLOTS = [upper_slots(step) for step in UNITS]
TABLE = np.array([upper_slots(step) for step in DIAGONALS], np.int32)
CODES = np.array([(s[0] + 1) * 9 + (s[1] + 1) * 3 + s[2] + 1 for s in UNITS + DIAGONALS], np.int32)


def halves(x):
    hi = x.astype(jnp.bfloat16)
    return hi, (x - hi.astype(jnp.float32)).astype(jnp.bfloat16)


def three(a_hi, a_lo, b_hi, b_lo):
    def dot(a, b):
        return lax.dot_general(a, b, (((1,), (0,)), ((), ())), preferred_element_type=jnp.float32)

    return dot(a_hi, b_hi) + (dot(a_hi, b_lo) + dot(a_lo, b_hi))


VMEM = pl.BlockSpec(memory_space=pltpu.VMEM)
SMEM = pl.BlockSpec(memory_space=pltpu.SMEM)
PARAMS = pltpu.CompilerParams(vmem_limit_bytes=48 * 1024 * 1024)


def mats(n):
    return jax.ShapeDtypeStruct((n, 2, J, J), jnp.float32)


def reals(n):
    return jax.ShapeDtypeStruct((n, J, J), jnp.float32)


def block(ref_hi, ref_lo, at, re, im, sign):
    for ref, part_re, part_im in zip((ref_hi, ref_lo), halves(re), halves(im)):
        ref[at, :J, :J] = part_re
        ref[at, :J, J:] = part_im
        ref[at, J:, :J] = -part_im if sign > 0 else part_im
        ref[at, J:, J:] = part_re if sign > 0 else -part_re


def left_kernel(u_ref, m_ref, v_ref, b_hi, b_lo):
    a_hi, a_lo = halves(jnp.concatenate([u_ref[0, 0].T, u_ref[0, 1].T], 1))
    for j in range(NB):
        block(b_hi, b_lo, j % 2, m_ref[0, j, 0], m_ref[0, j, 1], -1)
        made = three(a_hi, a_lo, b_hi[j % 2], b_lo[j % 2])
        v_ref[0, j, 0] = made[:, :J]
        v_ref[0, j, 1] = made[:, J:]


def left_products(own_u, local_m):
    return pl.pallas_call(
        left_kernel,
        grid=(4,),
        in_specs=[
            pl.BlockSpec((1, 2, J, J), lambda k: (k, 0, 0, 0)),
            pl.BlockSpec((1, NB, 2, J, J), lambda k: (k, 0, 0, 0, 0)),
        ],
        out_specs=pl.BlockSpec((1, NB, 2, J, J), lambda k: (k, 0, 0, 0, 0)),
        scratch_shapes=[
            pltpu.VMEM((2, 2 * J, 2 * J), jnp.bfloat16),
            pltpu.VMEM((2, 2 * J, 2 * J), jnp.bfloat16),
        ],
        out_shape=jax.ShapeDtypeStruct((4, NB, 2, J, J), jnp.float32),
        compiler_params=PARAMS,
        cost_estimate=pl.CostEstimate(flops=1 << 32, bytes_accessed=8 << 20, transcendentals=0),
        name="left_products",
    )(own_u, local_m)


def write_pair(p_ref, d_ref, at, left_re, left_im, right_re, right_im, b_hi, b_lo):
    a_hi, a_lo = halves(jnp.concatenate([left_re, left_im], 1))
    slot = at % 2
    block(b_hi, b_lo, slot, right_re, right_im, 1)
    made = three(a_hi, a_lo, b_hi[slot], b_lo[slot])
    eye = lax.broadcasted_iota(jnp.int32, (J, J), 0) == lax.broadcasted_iota(jnp.int32, (J, J), 1)
    p_ref[at, 0] = made[:, :J]
    p_ref[at, 1] = made[:, J:]
    j, k = at // 4, at % 4
    d_ref[0, j, k : k + 1, :] = jnp.sum(jnp.where(eye, made[:, :J], 0.0), 0, keepdims=True)
    d_ref[1, j, k : k + 1, :] = jnp.sum(jnp.where(eye, made[:, J:], 0.0), 0, keepdims=True)


def write_phases(row_data, first, d_ref, phase_ref, sums):
    for j in range(3):
        d_re, d_im = d_ref[0, j], d_ref[1, j]
        phase = jnp.arctan2(d_im, d_re)
        phase_ref[j] = phase
        weight = row_data[first + j, 0]
        along = jnp.sum(phase, 0, keepdims=True) * weight
        for c in range(3):
            sums[c] = sums[c] + along * row_data[first + j, 1 + c]
        spread = 1.0 - d_re * d_re - d_im * d_im + phase * phase
        sums[3] = sums[3] + weight * jnp.sum(spread, 0, keepdims=True)
    return jnp.concatenate(sums, 0)


def unit_kernel(rows, row_data, own_ref, x_ref, y_ref, z_ref, v_ref, p_ref, d_ref, phase_ref, sum_ref, b_hi, b_lo):
    found = {i: (own_ref, i) for i in range(4)}
    for ref, slots in ((x_ref, UNIT_SLOTS[0]), (y_ref, UNIT_SLOTS[1][2:]), (z_ref, UNIT_SLOTS[2][1::2])):
        found.update({slot: (ref, i) for i, slot in enumerate(slots)})
    for p in range(12):
        j, k = p // 4, p % 4
        ref, i = found[UNIT_SLOTS[j][k]]
        row = rows[j]
        write_pair(p_ref, d_ref, p, v_ref[k, row, 0], v_ref[k, row, 1], ref[i, 0], ref[i, 1], b_hi, b_lo)
    sum_ref[...] = write_phases(row_data, 0, d_ref, phase_ref, [jnp.zeros((1, J), jnp.float32)] * 4)


def diagonal_kernel(ends, rows, row_data, so_far_ref, *refs, any_sign):
    parts, rest = refs[: len(SIZES)], refs[len(SIZES) :]
    if any_sign:
        v_ref, far_ref, *rest = rest
    else:
        v_ref, *rest = rest
    p_ref, d_ref, phase_ref, sum_ref, slots, b_hi, b_lo = rest
    at = 0
    for ref, n in zip(parts, SIZES):
        slots[at : at + n] = ref[...]
        at += n
    for p in range(12):
        j, k = p // 4, p % 4
        low, up = ends[0, j, k], ends[1, j, k]
        if any_sign:
            left_re, left_im = far_ref[j, low, 0], far_ref[j, low, 1]
        else:
            row = rows[3 + j]
            left_re, left_im = v_ref[k, row, 0], v_ref[k, row, 1]
        write_pair(p_ref, d_ref, p, left_re, left_im, slots[up, 0], slots[up, 1], b_hi, b_lo)
    total = write_phases(row_data, 3, d_ref, phase_ref, [so_far_ref[i : i + 1] for i in range(4)])
    for i in range(NKX):
        sum_ref[i] = total


def product_call(kernel, name, tables, arrays, sum_shape, extra=()):
    return pl.pallas_call(
        kernel,
        in_specs=[SMEM] * len(tables) + [VMEM] * len(arrays),
        out_specs=[VMEM] * 4,
        out_shape=[mats(12)] + [jax.ShapeDtypeStruct(n + (J,), jnp.float32) for n in ((2, 3, 4), (3, 4), sum_shape)],
        scratch_shapes=[
            *extra,
            pltpu.VMEM((2, 2 * J, 2 * J), jnp.bfloat16),
            pltpu.VMEM((2, 2 * J, 2 * J), jnp.bfloat16),
        ],
        compiler_params=PARAMS,
        cost_estimate=pl.CostEstimate(flops=1 << 32, bytes_accessed=4 << 20, transcendentals=0),
        name=name,
    )(*tables, *arrays)


def unit_products(rows, row_data, own, x, y, z, v):
    return product_call(unit_kernel, "unit_products", [rows, row_data], [own, x, y, z, v], (4,))


def diagonal_products(ends, rows, row_data, so_far, parts, v, far=None):
    return product_call(
        functools.partial(diagonal_kernel, any_sign=far is not None),
        "diagonal_products",
        [ends, rows, row_data],
        [so_far, *parts, v] + ([] if far is None else [far]),
        (NKX, 4),
        [pltpu.VMEM((SLOTS, 2, J, J), jnp.float32)],
    )


def plain_and_cross(re, im, a, b):
    return re * a + im * b, im * a - re * b


def term_kernel(ends, row_data, pu_ref, du_ref, phu_ref, pd_ref, dd_ref, phd_ref, got_ref, *refs):
    total_ref, outs = refs[0], refs[1 : 1 + len(BACK)]
    plain, cross, rows_a, rows_b, turned_a, turned_b = refs[1 + len(BACK) :]
    total = jnp.sum(got_ref[...], 0)
    total_ref[...] = total
    centres = (-2.0 / NK) * total[:3]
    for j in range(NB):
        along = centres[0:1] * row_data[j, 1]
        for c in range(1, 3):
            along += centres[c : c + 1] * row_data[j, 1 + c]
        d_ref, phase_ref = (du_ref, phu_ref) if j < 3 else (dd_ref, phd_ref)
        d_re, d_im = d_ref[0, j % 3], d_ref[1, j % 3]
        ratio = (phase_ref[j % 3] + along) / (d_re * d_re + d_im * d_im)
        f_re = row_data[j, 0] * (d_re + ratio * d_im)
        f_im = row_data[j, 0] * (ratio * d_re - d_im)
        rows_a[4 * j : 4 * j + 4, :] = f_re + f_im
        rows_b[4 * j : 4 * j + 4, :] = f_re - f_im
    turned_a[...] = rows_a[...].T
    turned_b[...] = rows_b[...].T

    fixed = {slot: [] for slot in range(SLOTS)}
    for p in range(12):
        fixed[p % 4].append((p, True))
        fixed[UNIT_SLOTS[p // 4][p % 4]].append((p, False))
    step = J // 4
    for slot in range(SLOTS):
        for start in range(0, J, step):
            part = slice(start, start + step)
            sums = [jnp.zeros((step, J), jnp.float32)] * 2
            for p, starts_here in fixed[slot]:
                re, im = pu_ref[p, 0, part, :], pu_ref[p, 1, part, :]
                if starts_here:
                    a, b = rows_a[p : p + 1, :], rows_b[p : p + 1, :]
                    one, two = plain_and_cross(re, im, a, b)
                    sums = [sums[0] + one, sums[1] + two]
                else:
                    a, b = turned_a[part, p : p + 1], turned_b[part, p : p + 1]
                    one, two = plain_and_cross(re, im, a, b)
                    sums = [sums[0] - one, sums[1] - two]
            plain[slot, part, :], cross[slot, part, :] = sums
    for p in range(12):
        low, up = ends[0, p // 4, p % 4], ends[1, p // 4, p % 4]
        q = 12 + p
        for start in range(0, J, step):
            part = slice(start, start + step)
            re, im = pd_ref[p, 0, part, :], pd_ref[p, 1, part, :]
            one, two = plain_and_cross(re, im, rows_a[q : q + 1, :], rows_b[q : q + 1, :])
            plain[low, part, :] += one
            cross[low, part, :] += two
            one, two = plain_and_cross(re, im, turned_a[part, q : q + 1], turned_b[part, q : q + 1])
            plain[up, part, :] -= one
            cross[up, part, :] -= two
    at = 0
    for ref, n in zip(outs, BACK):
        for i in range(n):
            ref[i] = 2.0 * (plain[at] + cross[at].T)
            at += 1


def pair_terms(ends, row_data, unit, diagonal, got):
    return pl.pallas_call(
        term_kernel,
        in_specs=[SMEM, SMEM] + [VMEM] * 7,
        out_specs=[VMEM] * (1 + len(BACK)),
        out_shape=[jax.ShapeDtypeStruct((4, J), jnp.float32)] + [reals(n) for n in BACK],
        scratch_shapes=[pltpu.VMEM((SLOTS, J, J), jnp.float32)] * 2 + [pltpu.VMEM((J, J), jnp.float32)] * 4,
        compiler_params=PARAMS,
        cost_estimate=pl.CostEstimate(flops=1 << 24, bytes_accessed=8 << 20, transcendentals=0),
        name="pair_terms",
    )(ends, row_data, *unit, *diagonal, got)


def fold_kernel(own_ref, x_ref, y_ref, y_back_ref, z_ref, z_back_ref, g_ref):
    for k in range(4):
        total = own_ref[k] + x_ref[k]
        total += y_ref[k] if k < 2 else y_back_ref[k - 2]
        if k % 2 == 0:
            total += z_ref[k // 2]
        if k == 3:
            total += z_back_ref[0]
        turned = total.T
        g_ref[k, 0] = 0.5 * (total - turned)
        g_ref[k, 1] = 0.5 * (total + turned)


def fold_terms(*arrays):
    return pl.pallas_call(
        fold_kernel,
        in_specs=[VMEM] * len(arrays),
        out_specs=VMEM,
        out_shape=mats(4),
        compiler_params=PARAMS,
        name="fold_terms",
    )(*arrays)


def fetch(delta, *blocks):
    route = [(beside_device(i, delta), i) for i in range(NKX * NYZ)]
    return lax.ppermute(jnp.concatenate(blocks, 0), AXES, route)


def give_back(delta, block):
    route = [(i, beside_device(i, delta)) for i in range(NKX * NYZ)]
    return lax.ppermute(block, AXES, route)


X, Y, Y_BACK, Z, Z_BACK = (1, 0, 0), (0, 1, 0), (0, -1, 0), (0, 0, 1), (0, 0, -1)


def halo(own):
    y = fetch(Y, own[0:2])
    y_back = fetch(Y_BACK, own[2:4])
    x = fetch(X, own)
    z = fetch(Z, own[0::2])
    z_back = fetch(Z_BACK, own[3:4])
    xy = fetch(X, y, y_back)
    beside = fetch(Z, y[0:1], x[0::2])
    beside_back = fetch(Z_BACK, y[1:2], x[1::2])
    corner = fetch(Z, xy[0::2])
    corner_back = fetch(Z_BACK, xy[1::2])
    return own, x, y, xy, z, beside, z_back, beside_back, corner, corner_back


def fold_halo(own, x, y, xy, z, z_back, corner, corner_back):
    corner = give_back(Z, corner)
    corner_back = give_back(Z_BACK, corner_back)
    z = give_back(Z, z)
    z_back = give_back(Z_BACK, z_back)
    corners = [corner[0:1], corner_back[0:1], corner[1:2], corner_back[1:2]]
    xy = give_back(X, xy + jnp.concatenate(corners, 0))
    sides = [z[3:4], z_back[2:3], z[4:5], z_back[3:4]]
    x = give_back(X, x + jnp.concatenate(sides, 0))
    y = give_back(Y, y + xy[0:2] + jnp.concatenate([z[2:3], z_back[1:2]], 0))
    y_back = give_back(Y_BACK, xy[2:4])
    return fold_terms(own, x, y, y_back, z, z_back)


def over_all(copies):
    x = jnp.sum(lax.all_to_all(copies, "kx", 0, 0), 0)
    return lax.all_to_all(jnp.broadcast_to(x[None], (NYZ,) + x.shape), "kyz", 0, 0)


def on_device(intersections, rotations, offsets, weights, basis):
    own_u = rotations.reshape(4, 2, J, J)
    local_m = intersections.reshape(4, NB, 2, J, J)
    parts = halo(own_u)
    v = left_products(own_u, local_m)

    code = (offsets[:, 0] + 1) * 9 + (offsets[:, 1] + 1) * 3 + offsets[:, 2] + 1
    with_sign = jnp.asarray(CODES)[:, None] == code[None, :]
    against = 26 - jnp.asarray(CODES)[:, None] == code[None, :]
    here = with_sign | against
    rank = jnp.cumsum(jnp.any(here[3:], 1).astype(jnp.int32))
    nth = (rank[None] == jnp.arange(1, 4, dtype=jnp.int32)[:, None])[:, :, None] & here[None, 3:]
    chosen = jnp.concatenate([here[:3], jnp.any(nth, 1)], 0)
    rows = jnp.sum(jnp.where(chosen, jnp.arange(NB, dtype=jnp.int32)[None], 0), 1)
    upper = jnp.sum(jnp.where(jnp.any(nth, 2)[:, :, None], jnp.asarray(TABLE), 0), 1)
    lower = jnp.broadcast_to(jnp.arange(4, dtype=jnp.int32)[None], (3, 4))
    flipped = jnp.any(nth & against[None, 3:], (1, 2))
    ends = jnp.stack(
        [jnp.where(flipped[:, None], upper, lower), jnp.where(flipped[:, None], lower, upper)]
    )
    step_vec = jnp.sum(offsets.astype(jnp.float32)[:, :, None] * basis[None], 1)
    row_data = jnp.concatenate([weights[:, None], step_vec], 1)
    row_data = jnp.sum(jnp.where(chosen[:, :, None], row_data[None], 0.0), 1)

    *unit, so_far = unit_products(rows, row_data, own_u, parts[1], parts[2], parts[4], v)

    def usual(ends, rows, row_data, so_far, v, *parts):
        return diagonal_products(ends, rows, row_data, so_far, parts, v)

    def any_sign(ends, rows, row_data, so_far, v, *parts):
        far = [jnp.concatenate(halo(v[:, rows[j]]), 0) for j in range(3, NB)]
        return diagonal_products(ends, rows, row_data, so_far, parts, v, jnp.stack(far))

    *diagonal, part = lax.cond(
        jnp.any(flipped), any_sign, usual, ends, rows, row_data, so_far, v, *parts
    )
    got = over_all(part)
    total, *terms = pair_terms(ends, row_data, unit, diagonal, got)
    gradient = fold_halo(*terms)
    centres = (-2.0 / NK) * total[:3]
    spread = (2.0 / NK) * jnp.sum(total[3]) - jnp.sum(centres * centres)
    return gradient.reshape(1, 1, 2, 2, 2, J, J), centres, spread


def solution(mesh):
    placed = (
        P("kx", "kyz", None, None, None, None, None, None),
        P("kx", "kyz", None, None, None, None, None),
        P(),
        P(),
        P(),
    )
    return jax.shard_map(
        on_device,
        mesh=mesh,
        in_specs=placed,
        out_specs=(P("kx", "kyz", None, None, None, None, None), P(), P()),
        check_vma=False,
    )
```

```python
import functools

import jax
import jax.numpy as jnp
import numpy as np
from jax import lax
from jax.experimental import pallas as pl
from jax.experimental.pallas import tpu as pltpu
from jax.sharding import PartitionSpec as P

NB = 6
KZB = 4
J = 128
NKX = 8
NYZ = 32
NK = 1024
AXES = ("kx", "kyz")

UNITS = [(1, 0, 0), (0, 1, 0), (0, 0, 1)]
DIAGONALS = [
    (1, 1, 0),
    (1, -1, 0),
    (1, 0, 1),
    (1, 0, -1),
    (0, 1, 1),
    (0, 1, -1),
    (1, 1, 1),
    (1, 1, -1),
    (1, -1, 1),
    (1, -1, -1),
]
GRAY = [0, 1, 3, 2]
GROUPS = (
    [((0, 0, 0), t) for t in range(4)],
    [((1, 0, 0), t) for t in range(4)],
    [((0, 1, 0), 0), ((0, 1, 0), 1)],
    [((1, 1, 0), 0), ((1, 1, 0), 1), ((1, -1, 0), 2), ((1, -1, 0), 3)],
    [((0, 0, 1), 0), ((0, 0, 1), 2)],
    [((0, 1, 1), 0), ((1, 0, 1), 0), ((1, 0, 1), 2)],
    [((0, 0, -1), 3)],
    [((0, 1, -1), 1), ((1, 0, -1), 1), ((1, 0, -1), 3)],
    [((1, 1, 1), 0), ((1, -1, 1), 2)],
    [((1, 1, -1), 1), ((1, -1, -1), 3)],
)
SIZES = [len(group) for group in GROUPS]
SLOTS = sum(SIZES)
BACK = SIZES[:4] + [SIZES[4] + SIZES[5], SIZES[6] + SIZES[7]] + SIZES[8:]
SLOT_OF = {where: i for i, where in enumerate(sum(GROUPS, []))}


def place(step, k):
    row, col = k // 2 + step[1], k % 2 + step[2]
    return (step[0], row // 2, col // 2), (row % 2) * 2 + col % 2


def beside_device(device, delta):
    x, r = device // NYZ, device % NYZ
    x = (x + delta[0]) % NKX
    y = (r // 4 + delta[1]) % (NYZ // 4)
    g = (GRAY[r % 4] + delta[2]) % KZB
    return x * NYZ + y * 4 + GRAY[g]


def upper_slots(step):
    return [SLOT_OF[place(step, k)] for k in range(4)]


UNIT_SLOTS = [upper_slots(step) for step in UNITS]
TABLE = np.array([upper_slots(step) for step in DIAGONALS], np.int32)
CODES = np.array([(s[0] + 1) * 9 + (s[1] + 1) * 3 + s[2] + 1 for s in UNITS + DIAGONALS], np.int32)


def halves(x):
    hi = x.astype(jnp.bfloat16)
    return hi, (x - hi.astype(jnp.float32)).astype(jnp.bfloat16)


def three(a_hi, a_lo, b_hi, b_lo):
    def dot(a, b):
        return lax.dot_general(a, b, (((1,), (0,)), ((), ())), preferred_element_type=jnp.float32)

    return dot(a_hi, b_hi) + (dot(a_hi, b_lo) + dot(a_lo, b_hi))


VMEM = pl.BlockSpec(memory_space=pltpu.VMEM)
SMEM = pl.BlockSpec(memory_space=pltpu.SMEM)
PARAMS = pltpu.CompilerParams(vmem_limit_bytes=48 * 1024 * 1024)


def mats(n):
    return jax.ShapeDtypeStruct((n, 2, J, J), jnp.float32)


def reals(n):
    return jax.ShapeDtypeStruct((n, J, J), jnp.float32)


def block(ref_hi, ref_lo, at, re, im, sign):
    for ref, part_re, part_im in zip((ref_hi, ref_lo), halves(re), halves(im)):
        ref[at, :J, :J] = part_re
        ref[at, :J, J:] = part_im
        ref[at, J:, :J] = -part_im if sign > 0 else part_im
        ref[at, J:, J:] = part_re if sign > 0 else -part_re


def left_kernel(u_ref, m_ref, v_ref, b_hi, b_lo):
    a_hi, a_lo = halves(jnp.concatenate([u_ref[0, 0].T, u_ref[0, 1].T], 1))
    for j in range(NB):
        block(b_hi, b_lo, j % 2, m_ref[0, j, 0], m_ref[0, j, 1], -1)
        made = three(a_hi, a_lo, b_hi[j % 2], b_lo[j % 2])
        v_ref[0, j, 0] = made[:, :J]
        v_ref[0, j, 1] = made[:, J:]


def left_products(own_u, local_m):
    return pl.pallas_call(
        left_kernel,
        grid=(4,),
        in_specs=[
            pl.BlockSpec((1, 2, J, J), lambda k: (k, 0, 0, 0)),
            pl.BlockSpec((1, NB, 2, J, J), lambda k: (k, 0, 0, 0, 0)),
        ],
        out_specs=pl.BlockSpec((1, NB, 2, J, J), lambda k: (k, 0, 0, 0, 0)),
        scratch_shapes=[
            pltpu.VMEM((2, 2 * J, 2 * J), jnp.bfloat16),
            pltpu.VMEM((2, 2 * J, 2 * J), jnp.bfloat16),
        ],
        out_shape=jax.ShapeDtypeStruct((4, NB, 2, J, J), jnp.float32),
        compiler_params=PARAMS,
        cost_estimate=pl.CostEstimate(flops=1 << 32, bytes_accessed=8 << 20, transcendentals=0),
        name="left_products",
    )(own_u, local_m)


def write_pair(p_ref, d_ref, at, left_re, left_im, right_re, right_im, b_hi, b_lo):
    a_hi, a_lo = halves(jnp.concatenate([left_re, left_im], 1))
    slot = at % 2
    block(b_hi, b_lo, slot, right_re, right_im, 1)
    made = three(a_hi, a_lo, b_hi[slot], b_lo[slot])
    eye = lax.broadcasted_iota(jnp.int32, (J, J), 0) == lax.broadcasted_iota(jnp.int32, (J, J), 1)
    p_ref[at, 0] = made[:, :J]
    p_ref[at, 1] = made[:, J:]
    j, k = at // 4, at % 4
    d_ref[0, j, k : k + 1, :] = jnp.sum(jnp.where(eye, made[:, :J], 0.0), 0, keepdims=True)
    d_ref[1, j, k : k + 1, :] = jnp.sum(jnp.where(eye, made[:, J:], 0.0), 0, keepdims=True)


def write_phases(row_data, first, d_ref, phase_ref, sums):
    for j in range(3):
        d_re, d_im = d_ref[0, j], d_ref[1, j]
        phase = jnp.arctan2(d_im, d_re)
        phase_ref[j] = phase
        weight = row_data[first + j, 0]
        along = jnp.sum(phase, 0, keepdims=True) * weight
        for c in range(3):
            sums[c] = sums[c] + along * row_data[first + j, 1 + c]
        spread = 1.0 - d_re * d_re - d_im * d_im + phase * phase
        sums[3] = sums[3] + weight * jnp.sum(spread, 0, keepdims=True)
    return jnp.concatenate(sums, 0)


def unit_kernel(rows, row_data, own_ref, x_ref, y_ref, z_ref, v_ref, p_ref, d_ref, phase_ref, sum_ref, b_hi, b_lo):
    found = {i: (own_ref, i) for i in range(4)}
    for ref, slots in ((x_ref, UNIT_SLOTS[0]), (y_ref, UNIT_SLOTS[1][2:]), (z_ref, UNIT_SLOTS[2][1::2])):
        found.update({slot: (ref, i) for i, slot in enumerate(slots)})
    for p in range(12):
        j, k = p // 4, p % 4
        ref, i = found[UNIT_SLOTS[j][k]]
        row = rows[j]
        write_pair(p_ref, d_ref, p, v_ref[k, row, 0], v_ref[k, row, 1], ref[i, 0], ref[i, 1], b_hi, b_lo)
    sum_ref[...] = write_phases(row_data, 0, d_ref, phase_ref, [jnp.zeros((1, J), jnp.float32)] * 4)


def diagonal_kernel(ends, rows, row_data, so_far_ref, *refs, any_sign):
    parts, rest = refs[: len(SIZES)], refs[len(SIZES) :]
    if any_sign:
        v_ref, far_ref, *rest = rest
    else:
        v_ref, *rest = rest
    p_ref, d_ref, phase_ref, sum_ref, slots, b_hi, b_lo = rest
    at = 0
    for ref, n in zip(parts, SIZES):
        slots[at : at + n] = ref[...]
        at += n
    for p in range(12):
        j, k = p // 4, p % 4
        low, up = ends[0, j, k], ends[1, j, k]
        if any_sign:
            left_re, left_im = far_ref[low, j, 0], far_ref[low, j, 1]
        else:
            row = rows[3 + j]
            left_re, left_im = v_ref[k, row, 0], v_ref[k, row, 1]
        write_pair(p_ref, d_ref, p, left_re, left_im, slots[up, 0], slots[up, 1], b_hi, b_lo)
    total = write_phases(row_data, 3, d_ref, phase_ref, [so_far_ref[i : i + 1] for i in range(4)])
    for i in range(NKX):
        sum_ref[i] = total


def product_call(kernel, name, tables, arrays, sum_shape, extra=()):
    return pl.pallas_call(
        kernel,
        in_specs=[SMEM] * len(tables) + [VMEM] * len(arrays),
        out_specs=[VMEM] * 4,
        out_shape=[mats(12)] + [jax.ShapeDtypeStruct(n + (J,), jnp.float32) for n in ((2, 3, 4), (3, 4), sum_shape)],
        scratch_shapes=[
            *extra,
            pltpu.VMEM((2, 2 * J, 2 * J), jnp.bfloat16),
            pltpu.VMEM((2, 2 * J, 2 * J), jnp.bfloat16),
        ],
        compiler_params=PARAMS,
        cost_estimate=pl.CostEstimate(flops=1 << 32, bytes_accessed=4 << 20, transcendentals=0),
        name=name,
    )(*tables, *arrays)


def unit_products(rows, row_data, own, x, y, z, v):
    return product_call(unit_kernel, "unit_products", [rows, row_data], [own, x, y, z, v], (4,))


def diagonal_products(ends, rows, row_data, so_far, parts, v, far=None):
    return product_call(
        functools.partial(diagonal_kernel, any_sign=far is not None),
        "diagonal_products",
        [ends, rows, row_data],
        [so_far, *parts, v] + ([] if far is None else [far]),
        (NKX, 4),
        [pltpu.VMEM((SLOTS, 2, J, J), jnp.float32)],
    )


def plain_and_cross(re, im, a, b):
    return re * a + im * b, im * a - re * b


def term_kernel(ends, row_data, pu_ref, du_ref, phu_ref, pd_ref, dd_ref, phd_ref, got_ref, *refs):
    total_ref, outs = refs[0], refs[1 : 1 + len(BACK)]
    plain, cross, rows_a, rows_b, turned_a, turned_b = refs[1 + len(BACK) :]
    total = jnp.sum(got_ref[...], 0)
    total_ref[...] = total
    centres = (-2.0 / NK) * total[:3]
    for j in range(NB):
        along = centres[0:1] * row_data[j, 1]
        for c in range(1, 3):
            along += centres[c : c + 1] * row_data[j, 1 + c]
        d_ref, phase_ref = (du_ref, phu_ref) if j < 3 else (dd_ref, phd_ref)
        d_re, d_im = d_ref[0, j % 3], d_ref[1, j % 3]
        ratio = (phase_ref[j % 3] + along) / (d_re * d_re + d_im * d_im)
        f_re = row_data[j, 0] * (d_re + ratio * d_im)
        f_im = row_data[j, 0] * (ratio * d_re - d_im)
        rows_a[4 * j : 4 * j + 4, :] = f_re + f_im
        rows_b[4 * j : 4 * j + 4, :] = f_re - f_im
    turned_a[...] = rows_a[...].T
    turned_b[...] = rows_b[...].T

    fixed = {slot: [] for slot in range(SLOTS)}
    for p in range(12):
        fixed[p % 4].append((p, True))
        fixed[UNIT_SLOTS[p // 4][p % 4]].append((p, False))
    step = J // 4
    for slot in range(SLOTS):
        for start in range(0, J, step):
            part = slice(start, start + step)
            sums = [jnp.zeros((step, J), jnp.float32)] * 2
            for p, starts_here in fixed[slot]:
                re, im = pu_ref[p, 0, part, :], pu_ref[p, 1, part, :]
                if starts_here:
                    a, b = rows_a[p : p + 1, :], rows_b[p : p + 1, :]
                    one, two = plain_and_cross(re, im, a, b)
                    sums = [sums[0] + one, sums[1] + two]
                else:
                    a, b = turned_a[part, p : p + 1], turned_b[part, p : p + 1]
                    one, two = plain_and_cross(re, im, a, b)
                    sums = [sums[0] - one, sums[1] - two]
            plain[slot, part, :], cross[slot, part, :] = sums
    for p in range(12):
        low, up = ends[0, p // 4, p % 4], ends[1, p // 4, p % 4]
        q = 12 + p
        for start in range(0, J, step):
            part = slice(start, start + step)
            re, im = pd_ref[p, 0, part, :], pd_ref[p, 1, part, :]
            one, two = plain_and_cross(re, im, rows_a[q : q + 1, :], rows_b[q : q + 1, :])
            plain[low, part, :] += one
            cross[low, part, :] += two
            one, two = plain_and_cross(re, im, turned_a[part, q : q + 1], turned_b[part, q : q + 1])
            plain[up, part, :] -= one
            cross[up, part, :] -= two
    at = 0
    for ref, n in zip(outs, BACK):
        for i in range(n):
            ref[i] = 2.0 * (plain[at] + cross[at].T)
            at += 1


def pair_terms(ends, row_data, unit, diagonal, got):
    return pl.pallas_call(
        term_kernel,
        in_specs=[SMEM, SMEM] + [VMEM] * 7,
        out_specs=[VMEM] * (1 + len(BACK)),
        out_shape=[jax.ShapeDtypeStruct((4, J), jnp.float32)] + [reals(n) for n in BACK],
        scratch_shapes=[pltpu.VMEM((SLOTS, J, J), jnp.float32)] * 2 + [pltpu.VMEM((J, J), jnp.float32)] * 4,
        compiler_params=PARAMS,
        cost_estimate=pl.CostEstimate(flops=1 << 24, bytes_accessed=8 << 20, transcendentals=0),
        name="pair_terms",
    )(ends, row_data, *unit, *diagonal, got)


def fold_kernel(own_ref, x_ref, y_ref, y_back_ref, z_ref, z_back_ref, g_ref):
    for k in range(4):
        total = own_ref[k] + x_ref[k]
        total += y_ref[k] if k < 2 else y_back_ref[k - 2]
        if k % 2 == 0:
            total += z_ref[k // 2]
        if k == 3:
            total += z_back_ref[0]
        turned = total.T
        g_ref[k, 0] = 0.5 * (total - turned)
        g_ref[k, 1] = 0.5 * (total + turned)


def fold_terms(*arrays):
    return pl.pallas_call(
        fold_kernel,
        in_specs=[VMEM] * len(arrays),
        out_specs=VMEM,
        out_shape=mats(4),
        compiler_params=PARAMS,
        name="fold_terms",
    )(*arrays)


def fetch(delta, *blocks):
    route = [(beside_device(i, delta), i) for i in range(NKX * NYZ)]
    return lax.ppermute(jnp.concatenate(blocks, 0), AXES, route)


def give_back(delta, block):
    route = [(i, beside_device(i, delta)) for i in range(NKX * NYZ)]
    return lax.ppermute(block, AXES, route)


X, Y, Y_BACK, Z, Z_BACK = (1, 0, 0), (0, 1, 0), (0, -1, 0), (0, 0, 1), (0, 0, -1)


def halo(own):
    y = fetch(Y, own[0:2])
    y_back = fetch(Y_BACK, own[2:4])
    x = fetch(X, own)
    z = fetch(Z, own[0::2])
    z_back = fetch(Z_BACK, own[3:4])
    xy = fetch(X, y, y_back)
    beside = fetch(Z, y[0:1], x[0::2])
    beside_back = fetch(Z_BACK, y[1:2], x[1::2])
    corner = fetch(Z, xy[0::2])
    corner_back = fetch(Z_BACK, xy[1::2])
    return own, x, y, xy, z, beside, z_back, beside_back, corner, corner_back


def fold_halo(own, x, y, xy, z, z_back, corner, corner_back):
    corner = give_back(Z, corner)
    corner_back = give_back(Z_BACK, corner_back)
    z = give_back(Z, z)
    z_back = give_back(Z_BACK, z_back)
    corners = [corner[0:1], corner_back[0:1], corner[1:2], corner_back[1:2]]
    xy = give_back(X, xy + jnp.concatenate(corners, 0))
    sides = [z[3:4], z_back[2:3], z[4:5], z_back[3:4]]
    x = give_back(X, x + jnp.concatenate(sides, 0))
    y = give_back(Y, y + xy[0:2] + jnp.concatenate([z[2:3], z_back[1:2]], 0))
    y_back = give_back(Y_BACK, xy[2:4])
    return fold_terms(own, x, y, y_back, z, z_back)


def over_all(copies):
    x = jnp.sum(lax.all_to_all(copies, "kx", 0, 0), 0)
    return lax.all_to_all(jnp.broadcast_to(x[None], (NYZ,) + x.shape), "kyz", 0, 0)


def on_device(intersections, rotations, offsets, weights, basis):
    own_u = rotations.reshape(4, 2, J, J)
    local_m = intersections.reshape(4, NB, 2, J, J)
    parts = halo(own_u)
    v = left_products(own_u, local_m)

    code = (offsets[:, 0] + 1) * 9 + (offsets[:, 1] + 1) * 3 + offsets[:, 2] + 1
    with_sign = jnp.asarray(CODES)[:, None] == code[None, :]
    against = 26 - jnp.asarray(CODES)[:, None] == code[None, :]
    here = with_sign | against
    rank = jnp.cumsum(jnp.any(here[3:], 1).astype(jnp.int32))
    nth = (rank[None] == jnp.arange(1, 4, dtype=jnp.int32)[:, None])[:, :, None] & here[None, 3:]
    chosen = jnp.concatenate([here[:3], jnp.any(nth, 1)], 0)
    rows = jnp.sum(jnp.where(chosen, jnp.arange(NB, dtype=jnp.int32)[None], 0), 1)
    upper = jnp.sum(jnp.where(jnp.any(nth, 2)[:, :, None], jnp.asarray(TABLE), 0), 1)
    lower = jnp.broadcast_to(jnp.arange(4, dtype=jnp.int32)[None], (3, 4))
    flipped = jnp.any(nth & against[None, 3:], (1, 2))
    ends = jnp.stack(
        [jnp.where(flipped[:, None], upper, lower), jnp.where(flipped[:, None], lower, upper)]
    )
    step_vec = jnp.sum(offsets.astype(jnp.float32)[:, :, None] * basis[None], 1)
    row_data = jnp.concatenate([weights[:, None], step_vec], 1)
    row_data = jnp.sum(jnp.where(chosen[:, :, None], row_data[None], 0.0), 1)

    *unit, so_far = unit_products(rows, row_data, own_u, parts[1], parts[2], parts[4], v)

    def usual(ends, rows, row_data, so_far, v, *parts):
        return diagonal_products(ends, rows, row_data, so_far, parts, v)

    def any_sign(ends, rows, row_data, so_far, v, *parts):
        far = halo(jnp.stack([v[:, rows[j]] for j in range(3, NB)], 1))
        return diagonal_products(ends, rows, row_data, so_far, parts, v, jnp.concatenate(far, 0))

    *diagonal, part = lax.cond(
        jnp.any(flipped), any_sign, usual, ends, rows, row_data, so_far, v, *parts
    )
    got = over_all(part)
    total, *terms = pair_terms(ends, row_data, unit, diagonal, got)
    gradient = fold_halo(*terms)
    centres = (-2.0 / NK) * total[:3]
    spread = (2.0 / NK) * jnp.sum(total[3]) - jnp.sum(centres * centres)
    return gradient.reshape(1, 1, 2, 2, 2, J, J), centres, spread


def solution(mesh):
    placed = (
        P("kx", "kyz", None, None, None, None, None, None),
        P("kx", "kyz", None, None, None, None, None),
        P(),
        P(),
        P(),
    )
    return jax.shard_map(
        on_device,
        mesh=mesh,
        in_specs=placed,
        out_specs=(P("kx", "kyz", None, None, None, None, None), P(), P()),
        check_vma=False,
    )
```

```python
import functools

import jax
import jax.numpy as jnp
from jax import lax
from jax.experimental import pallas as pl
from jax.experimental.pallas import tpu as pltpu
from jax.sharding import PartitionSpec as P

NB = 6
KZB = 4
J = 128
NKX = 8
NYZ = 32
NK = 1024
AXES = ("kx", "kyz")

UNITS = [(1, 0, 0), (0, 1, 0), (0, 0, 1)]
DIAGONALS = [
    (1, 1, 0),
    (1, -1, 0),
    (1, 0, 1),
    (1, 0, -1),
    (0, 1, 1),
    (0, 1, -1),
    (1, 1, 1),
    (1, 1, -1),
    (1, -1, 1),
    (1, -1, -1),
]
GRAY = [0, 1, 3, 2]
GROUPS = (
    [((0, 0, 0), t) for t in range(4)],
    [((1, 0, 0), t) for t in range(4)],
    [((0, 1, 0), 0), ((0, 1, 0), 1)],
    [((1, 1, 0), 0), ((1, 1, 0), 1), ((1, -1, 0), 2), ((1, -1, 0), 3)],
    [((0, 0, 1), 0), ((0, 0, 1), 2)],
    [((0, 1, 1), 0), ((1, 0, 1), 0), ((1, 0, 1), 2)],
    [((0, 0, -1), 3)],
    [((0, 1, -1), 1), ((1, 0, -1), 1), ((1, 0, -1), 3)],
    [((0, 0, -1), 3), ((0, 0, -1), 1)],
    [((0, 0, 1), 2), ((0, 0, 1), 0)],
)
SIZES = [len(group) for group in GROUPS]
SLOTS = sum(SIZES)
CORNER = SLOTS - 4
SLOT_OF = {where: i for i, where in enumerate(sum(GROUPS, [])[:CORNER])}


def place(step, k):
    row, col = k // 2 + step[1], k % 2 + step[2]
    return (step[0], row // 2, col // 2), (row % 2) * 2 + col % 2


def beside_device(device, delta):
    x, r = device // NYZ, device % NYZ
    x = (x + delta[0]) % NKX
    y = (r // 4 + delta[1]) % (NYZ // 4)
    g = (GRAY[r % 4] + delta[2]) % KZB
    return x * NYZ + y * 4 + GRAY[g]


def pair_slots(step, corner):
    lower, upper = [], []
    for k in range(4):
        (dx, dy, dz), t = place(step, k)
        if dx and dy and dz:
            lower.append(CORNER + corner)
            upper.append(SLOT_OF[((dx, dy, 0), t)])
        else:
            lower.append(k)
            upper.append(SLOT_OF[((dx, dy, dz), t)])
    return lower, upper


CORNERS = [(1, 1, 1), (1, -1, 1), (1, 1, -1), (1, -1, -1)]
UNIT_SLOTS = [pair_slots(step, 0)[1] for step in UNITS]
TABLE = [pair_slots(step, CORNERS.index(step) if step in CORNERS else 0) for step in DIAGONALS]
CODES = [(s[0] + 1) * 9 + (s[1] + 1) * 3 + s[2] + 1 for s in UNITS + DIAGONALS]


def halves(x):
    hi = x.astype(jnp.bfloat16)
    return hi, (x - hi.astype(jnp.float32)).astype(jnp.bfloat16)


def three(a_hi, a_lo, b_hi, b_lo):
    def dot(a, b):
        return lax.dot_general(a, b, (((1,), (0,)), ((), ())), preferred_element_type=jnp.float32)

    return dot(a_hi, b_hi) + (dot(a_hi, b_lo) + dot(a_lo, b_hi))


VMEM = pl.BlockSpec(memory_space=pltpu.VMEM)
SMEM = pl.BlockSpec(memory_space=pltpu.SMEM)
PARAMS = pltpu.CompilerParams(vmem_limit_bytes=48 * 1024 * 1024)


def mats(n):
    return jax.ShapeDtypeStruct((n, 2, J, J), jnp.float32)


def reals(n):
    return jax.ShapeDtypeStruct((n, J, J), jnp.float32)


def block(ref_hi, ref_lo, at, re, im, sign):
    for ref, part_re, part_im in zip((ref_hi, ref_lo), halves(re), halves(im)):
        ref[at, :J, :J] = part_re
        ref[at, :J, J:] = part_im
        ref[at, J:, :J] = -part_im if sign > 0 else part_im
        ref[at, J:, J:] = part_re if sign > 0 else -part_re


def plan_kernel(offsets, weights, basis, rows, corner_rows, ends, row_data, flipped):
    codes = [(offsets[r, 0] + 1) * 9 + (offsets[r, 1] + 1) * 3 + offsets[r, 2] + 1 for r in range(NB)]
    for j in range(NB):
        rows[j] = 0
    for i in range(3):
        for k in range(4):
            ends[0, i, k] = k
            ends[1, i, k] = k
    count, any_flip = 0, 0
    for i, code in enumerate(CODES):
        row, found, flip = 0, 0, 0
        for r in range(NB):
            along, against = codes[r] == code, codes[r] == 26 - code
            row += jnp.where(along | against, r, 0)
            found += jnp.where(along | against, 1, 0)
            flip += jnp.where(against, 1, 0)
        if i < 3:
            rows[i] = row
            continue
        if DIAGONALS[i - 3] in CORNERS:
            corner_rows[CORNERS.index(DIAGONALS[i - 3])] = row
        place_at = jnp.minimum(count, 2)

        @pl.when(found > 0)
        def _():
            rows[3 + place_at] = row
            lower, upper = TABLE[i - 3]
            for k in range(4):
                ends[0, place_at, k] = jnp.where(flip > 0, upper[k], lower[k])
                ends[1, place_at, k] = jnp.where(flip > 0, lower[k], upper[k])

        count += found
        any_flip += flip
    flipped[0] = any_flip
    for j in range(NB):
        row = rows[j]
        row_data[j, 0] = weights[row]
        for c in range(3):
            step = offsets[row, 0].astype(jnp.float32) * basis[0, c]
            for x in range(1, 3):
                step += offsets[row, x].astype(jnp.float32) * basis[x, c]
            row_data[j, 1 + c] = step


def make_rows(offsets, weights, basis):
    whole = jnp.int32, jnp.float32
    shapes = [((NB,), 0), ((4,), 0), ((2, 3, 4), 0), ((NB, 4), 1), ((1,), 0)]
    return pl.pallas_call(
        plan_kernel,
        in_specs=[SMEM] * 3,
        out_specs=[SMEM] * len(shapes),
        out_shape=[jax.ShapeDtypeStruct(shape, whole[kind]) for shape, kind in shapes],
        name="make_rows",
    )(offsets, weights, basis)


def left_kernel(corner_rows, u_ref, m_ref, v_ref, corner_ref, b_hi, b_lo):
    a_hi, a_lo = halves(jnp.concatenate([u_ref[0, 0].T, u_ref[0, 1].T], 1))
    for j in range(NB):
        block(b_hi, b_lo, j % 2, m_ref[0, j, 0], m_ref[0, j, 1], -1)
        made = three(a_hi, a_lo, b_hi[j % 2], b_lo[j % 2])
        v_ref[0, j, 0] = made[:, :J]
        v_ref[0, j, 1] = made[:, J:]
    corner_ref[0] = v_ref[0, corner_rows[corner_of(pl.program_id(0))]]


def corner_of(k):
    return jnp.where(k == 3, 0, jnp.where(k == 1, 1, jnp.where(k == 2, 2, 3)))


def left_products(corner_rows, own_u, local_m):
    return pl.pallas_call(
        left_kernel,
        grid=(4,),
        in_specs=[
            SMEM,
            pl.BlockSpec((1, 2, J, J), lambda k: (k, 0, 0, 0)),
            pl.BlockSpec((1, NB, 2, J, J), lambda k: (k, 0, 0, 0, 0)),
        ],
        out_specs=[
            pl.BlockSpec((1, NB, 2, J, J), lambda k: (k, 0, 0, 0, 0)),
            pl.BlockSpec((1, 2, J, J), lambda k: (corner_of(k), 0, 0, 0)),
        ],
        scratch_shapes=[
            pltpu.VMEM((2, 2 * J, 2 * J), jnp.bfloat16),
            pltpu.VMEM((2, 2 * J, 2 * J), jnp.bfloat16),
        ],
        out_shape=[jax.ShapeDtypeStruct((4, NB, 2, J, J), jnp.float32), mats(4)],
        compiler_params=PARAMS,
        cost_estimate=pl.CostEstimate(flops=1 << 32, bytes_accessed=8 << 20, transcendentals=0),
        name="left_products",
    )(corner_rows, own_u, local_m)


def write_pair(p_ref, d_ref, at, left_re, left_im, right_re, right_im, b_hi, b_lo):
    a_hi, a_lo = halves(jnp.concatenate([left_re, left_im], 1))
    slot = at % 2
    block(b_hi, b_lo, slot, right_re, right_im, 1)
    made = three(a_hi, a_lo, b_hi[slot], b_lo[slot])
    eye = lax.broadcasted_iota(jnp.int32, (J, J), 0) == lax.broadcasted_iota(jnp.int32, (J, J), 1)
    p_ref[at, 0] = made[:, :J]
    p_ref[at, 1] = made[:, J:]
    j, k = at // 4, at % 4
    d_ref[0, j, k : k + 1, :] = jnp.sum(jnp.where(eye, made[:, :J], 0.0), 0, keepdims=True)
    d_ref[1, j, k : k + 1, :] = jnp.sum(jnp.where(eye, made[:, J:], 0.0), 0, keepdims=True)


def write_phases(row_data, first, d_ref, phase_ref, sums):
    for j in range(3):
        d_re, d_im = d_ref[0, j], d_ref[1, j]
        phase = jnp.arctan2(d_im, d_re)
        phase_ref[j] = phase
        weight = row_data[first + j, 0]
        along = jnp.sum(phase, 0, keepdims=True) * weight
        for c in range(3):
            sums[c] = sums[c] + along * row_data[first + j, 1 + c]
        spread = 1.0 - d_re * d_re - d_im * d_im + phase * phase
        sums[3] = sums[3] + weight * jnp.sum(spread, 0, keepdims=True)
    return jnp.concatenate(sums, 0)


def unit_kernel(rows, row_data, own_ref, x_ref, y_ref, z_ref, v_ref, p_ref, d_ref, phase_ref, sum_ref, b_hi, b_lo):
    found = {i: (own_ref, i) for i in range(4)}
    for ref, slots in ((x_ref, UNIT_SLOTS[0]), (y_ref, UNIT_SLOTS[1][2:]), (z_ref, UNIT_SLOTS[2][1::2])):
        found.update({slot: (ref, i) for i, slot in enumerate(slots)})
    for p in range(12):
        j, k = p // 4, p % 4
        ref, i = found[UNIT_SLOTS[j][k]]
        row = rows[j]
        write_pair(p_ref, d_ref, p, v_ref[k, row, 0], v_ref[k, row, 1], ref[i, 0], ref[i, 1], b_hi, b_lo)
    sum_ref[...] = write_phases(row_data, 0, d_ref, phase_ref, [jnp.zeros((1, J), jnp.float32)] * 4)


def diagonal_kernel(ends, rows, row_data, so_far_ref, *refs, any_sign):
    sizes = SIZES if any_sign else SIZES[:-2]
    parts, rest = refs[: len(sizes)], refs[len(sizes) :]
    if any_sign:
        v_ref, far_ref, *rest = rest
    else:
        v_ref, corner_ref, *rest = rest
    p_ref, d_ref, phase_ref, sum_ref, slots, b_hi, b_lo = rest
    at = 0
    for ref, n in zip(parts, sizes):
        slots[at : at + n] = ref[...]
        at += n
    for p in range(12):
        j, k = p // 4, p % 4
        low, up = ends[0, j, k], ends[1, j, k]
        if any_sign:
            left_re, left_im = far_ref[low, j, 0], far_ref[low, j, 1]
        else:
            row, here = rows[3 + j], low < 4
            own, got = jnp.minimum(low, 3), jnp.maximum(low - CORNER, 0)
            left_re = jnp.where(here, v_ref[own, row, 0], corner_ref[got, 0])
            left_im = jnp.where(here, v_ref[own, row, 1], corner_ref[got, 1])
        write_pair(p_ref, d_ref, p, left_re, left_im, slots[up, 0], slots[up, 1], b_hi, b_lo)
    total = write_phases(row_data, 3, d_ref, phase_ref, [so_far_ref[i : i + 1] for i in range(4)])
    for i in range(NKX):
        sum_ref[i] = total


def product_call(kernel, name, tables, arrays, sum_shape, extra=()):
    return pl.pallas_call(
        kernel,
        in_specs=[SMEM] * len(tables) + [VMEM] * len(arrays),
        out_specs=[VMEM] * 4,
        out_shape=[mats(12)] + [jax.ShapeDtypeStruct(n + (J,), jnp.float32) for n in ((2, 3, 4), (3, 4), sum_shape)],
        scratch_shapes=[
            *extra,
            pltpu.VMEM((2, 2 * J, 2 * J), jnp.bfloat16),
            pltpu.VMEM((2, 2 * J, 2 * J), jnp.bfloat16),
        ],
        compiler_params=PARAMS,
        cost_estimate=pl.CostEstimate(flops=1 << 32, bytes_accessed=4 << 20, transcendentals=0),
        name=name,
    )(*tables, *arrays)


def unit_products(rows, row_data, own, x, y, z, v):
    return product_call(unit_kernel, "unit_products", [rows, row_data], [own, x, y, z, v], (4,))


def diagonal_products(ends, rows, row_data, so_far, parts, v, corner_v, far=None):
    return product_call(
        functools.partial(diagonal_kernel, any_sign=far is not None),
        "diagonal_products",
        [ends, rows, row_data],
        [so_far, *parts, v] + ([corner_v] if far is None else [far]),
        (NKX, 4),
        [pltpu.VMEM((SLOTS, 2, J, J), jnp.float32)],
    )


def plain_and_cross(re, im, a, b):
    return re * a + im * b, im * a - re * b


def term_kernel(ends, row_data, pu_ref, du_ref, phu_ref, pd_ref, dd_ref, phd_ref, got_ref, *refs):
    total_ref, outs = refs[0], refs[1 : 1 + len(SIZES)]
    plain, cross, rows_a, rows_b, turned_a, turned_b = refs[1 + len(SIZES) :]
    total = jnp.sum(got_ref[...], 0)
    total_ref[...] = total
    centres = (-2.0 / NK) * total[:3]
    for j in range(NB):
        along = centres[0:1] * row_data[j, 1]
        for c in range(1, 3):
            along += centres[c : c + 1] * row_data[j, 1 + c]
        d_ref, phase_ref = (du_ref, phu_ref) if j < 3 else (dd_ref, phd_ref)
        d_re, d_im = d_ref[0, j % 3], d_ref[1, j % 3]
        ratio = (phase_ref[j % 3] + along) / (d_re * d_re + d_im * d_im)
        f_re = row_data[j, 0] * (d_re + ratio * d_im)
        f_im = row_data[j, 0] * (ratio * d_re - d_im)
        rows_a[4 * j : 4 * j + 4, :] = f_re + f_im
        rows_b[4 * j : 4 * j + 4, :] = f_re - f_im
    turned_a[...] = rows_a[...].T
    turned_b[...] = rows_b[...].T

    fixed = {slot: [] for slot in range(SLOTS)}
    for p in range(12):
        fixed[p % 4].append((p, True))
        fixed[UNIT_SLOTS[p // 4][p % 4]].append((p, False))
    step = J // 4
    for slot in range(SLOTS):
        for start in range(0, J, step):
            part = slice(start, start + step)
            sums = [jnp.zeros((step, J), jnp.float32)] * 2
            for p, starts_here in fixed[slot]:
                re, im = pu_ref[p, 0, part, :], pu_ref[p, 1, part, :]
                if starts_here:
                    a, b = rows_a[p : p + 1, :], rows_b[p : p + 1, :]
                    one, two = plain_and_cross(re, im, a, b)
                    sums = [sums[0] + one, sums[1] + two]
                else:
                    a, b = turned_a[part, p : p + 1], turned_b[part, p : p + 1]
                    one, two = plain_and_cross(re, im, a, b)
                    sums = [sums[0] - one, sums[1] - two]
            plain[slot, part, :], cross[slot, part, :] = sums
    for p in range(12):
        low, up = ends[0, p // 4, p % 4], ends[1, p // 4, p % 4]
        q = 12 + p
        for start in range(0, J, step):
            part = slice(start, start + step)
            re, im = pd_ref[p, 0, part, :], pd_ref[p, 1, part, :]
            one, two = plain_and_cross(re, im, rows_a[q : q + 1, :], rows_b[q : q + 1, :])
            plain[low, part, :] += one
            cross[low, part, :] += two
            one, two = plain_and_cross(re, im, turned_a[part, q : q + 1], turned_b[part, q : q + 1])
            plain[up, part, :] -= one
            cross[up, part, :] -= two
    at = 0
    for ref, n in zip(outs, SIZES):
        for i in range(n):
            ref[i] = 2.0 * (plain[at] + cross[at].T)
            at += 1


def pair_terms(ends, row_data, unit, diagonal, got):
    return pl.pallas_call(
        term_kernel,
        in_specs=[SMEM, SMEM] + [VMEM] * 7,
        out_specs=[VMEM] * (1 + len(SIZES)),
        out_shape=[jax.ShapeDtypeStruct((4, J), jnp.float32)] + [reals(n) for n in SIZES],
        scratch_shapes=[pltpu.VMEM((SLOTS, J, J), jnp.float32)] * 2 + [pltpu.VMEM((J, J), jnp.float32)] * 4,
        compiler_params=PARAMS,
        cost_estimate=pl.CostEstimate(flops=1 << 24, bytes_accessed=8 << 20, transcendentals=0),
        name="pair_terms",
    )(ends, row_data, *unit, *diagonal, got)


def fold_kernel(own_ref, x_ref, y_ref, y_back_ref, z_ref, z_back_ref, g_ref):
    for k in range(4):
        total = own_ref[k] + x_ref[k]
        total += y_ref[k] if k < 2 else y_back_ref[k - 2]
        if k == 0:
            total += z_ref[0] + z_ref[3]
        elif k == 1:
            total += z_back_ref[2]
        elif k == 2:
            total += z_ref[1] + z_ref[2]
        else:
            total += z_back_ref[0] + z_back_ref[1]
        turned = total.T
        g_ref[k, 0] = 0.5 * (total - turned)
        g_ref[k, 1] = 0.5 * (total + turned)


def fold_terms(*arrays):
    return pl.pallas_call(
        fold_kernel,
        in_specs=[VMEM] * len(arrays),
        out_specs=VMEM,
        out_shape=mats(4),
        compiler_params=PARAMS,
        name="fold_terms",
    )(*arrays)


def fetch(delta, *blocks):
    route = [(beside_device(i, delta), i) for i in range(NKX * NYZ)]
    return lax.ppermute(jnp.concatenate(blocks, 0), AXES, route)


def give_back(delta, block):
    route = [(i, beside_device(i, delta)) for i in range(NKX * NYZ)]
    return lax.ppermute(block, AXES, route)


X, Y, Y_BACK, Z, Z_BACK = (1, 0, 0), (0, 1, 0), (0, -1, 0), (0, 0, 1), (0, 0, -1)


def halo(own):
    y = fetch(Y, own[0:2])
    y_back = fetch(Y_BACK, own[2:4])
    x = fetch(X, own)
    z = fetch(Z, own[0::2])
    z_back = fetch(Z_BACK, own[3:4])
    xy = fetch(X, y, y_back)
    beside = fetch(Z, y[0:1], x[0::2])
    beside_back = fetch(Z_BACK, y[1:2], x[1::2])
    return own, x, y, xy, z, beside, z_back, beside_back


def corners(field):
    return fetch(Z_BACK, field[0:2]), fetch(Z, field[2:4])


def fold_halo(own, x, y, xy, z, beside, z_back, beside_back, corner, corner_back):
    xy = give_back(X, xy)
    beside = give_back(Z, beside)
    beside_back = give_back(Z_BACK, beside_back)
    sides = [beside[1:2], beside_back[1:2], beside[2:3], beside_back[2:3]]
    x = give_back(X, x + jnp.concatenate(sides, 0))
    beside, z, corner_back, z_back, corner = lax.optimization_barrier(
        (beside, z, corner_back, z_back, corner)
    )
    z = give_back(Z, jnp.concatenate([z, corner_back], 0))
    z_back = give_back(Z_BACK, jnp.concatenate([z_back, corner], 0))
    y = give_back(Y, y + xy[0:2] + jnp.concatenate([beside[0:1], beside_back[0:1]], 0))
    y_back = give_back(Y_BACK, xy[2:4])
    return fold_terms(own, x, y, y_back, z, z_back)


def over_all(copies):
    x = copies[0] + lax.ppermute(copies[0], "kyz", [(i, i ^ 1) for i in range(NYZ)])
    one_core = [[core + 2 * i for i in range(NYZ // 2)] for core in range(2)]
    copies = jnp.broadcast_to(x[None], (NYZ // 2,) + x.shape)
    x = jnp.sum(lax.all_to_all(copies, "kyz", 0, 0, axis_index_groups=one_core), 0)
    copies = jnp.broadcast_to(x[None], (NKX,) + x.shape)
    return lax.all_to_all(copies, "kx", 0, 0)


def on_device(intersections, rotations, offsets, weights, basis):
    own_u = rotations.reshape(4, 2, J, J)
    local_m = intersections.reshape(4, NB, 2, J, J)
    parts = halo(own_u)
    rows, corner_rows, ends, row_data, flipped = make_rows(offsets, weights, basis)
    v, corner_v = left_products(corner_rows, own_u, local_m)
    *unit, so_far = unit_products(rows, row_data, own_u, parts[1], parts[2], parts[4], v)

    corner_v, _ = lax.optimization_barrier((corner_v, parts[1]))
    corner_v = jnp.concatenate(corners(corner_v), 0)

    def usual(ends, rows, row_data, so_far, v, corner_v, *parts):
        return diagonal_products(ends, rows, row_data, so_far, parts, v, corner_v)

    def any_sign(ends, rows, row_data, so_far, v, corner_v, *parts):
        own_v = jnp.stack([v[:, rows[j]] for j in range(3, NB)], 1)
        own = jnp.concatenate([parts[0][:, None], own_v], 1)
        low = corners(jnp.concatenate([own[3:4], own[1:3], own[0:1]], 0))
        far = jnp.concatenate(halo(own_v) + tuple(block[:, 1:] for block in low), 0)
        parts += tuple(block[:, 0] for block in low)
        return diagonal_products(ends, rows, row_data, so_far, parts, v, corner_v, far)

    *diagonal, part = lax.cond(
        flipped[0] > 0, any_sign, usual, ends, rows, row_data, so_far, v, corner_v, *parts
    )
    got = over_all(part)
    total, *terms = pair_terms(ends, row_data, unit, diagonal, got)
    gradient = fold_halo(*terms)
    centres = (-2.0 / NK) * total[:3]
    spread = (2.0 / NK) * jnp.sum(total[3]) - jnp.sum(centres * centres)
    return gradient.reshape(1, 1, 2, 2, 2, J, J), centres, spread


def solution(mesh):
    placed = (
        P("kx", "kyz", None, None, None, None, None, None),
        P("kx", "kyz", None, None, None, None, None),
        P(),
        P(),
        P(),
    )
    return jax.shard_map(
        on_device,
        mesh=mesh,
        in_specs=placed,
        out_specs=(P("kx", "kyz", None, None, None, None, None), P(), P()),
        check_vma=False,
    )
```

```python
import functools

import jax
import jax.numpy as jnp
from jax import lax
from jax.experimental import pallas as pl
from jax.experimental.pallas import tpu as pltpu
from jax.sharding import PartitionSpec as P

NB = 6
KZB = 4
J = 128
NKX = 8
NYZ = 32
NK = 1024
AXES = ("kx", "kyz")

UNITS = [(1, 0, 0), (0, 1, 0), (0, 0, 1)]
DIAGONALS = [
    (1, 1, 0),
    (1, -1, 0),
    (1, 0, 1),
    (1, 0, -1),
    (0, 1, 1),
    (0, 1, -1),
    (1, 1, 1),
    (1, 1, -1),
    (1, -1, 1),
    (1, -1, -1),
]
GRAY = [0, 1, 3, 2]
GROUPS = (
    [((0, 0, 0), t) for t in range(4)],
    [((1, 0, 0), t) for t in range(4)],
    [((0, 1, 0), 0), ((0, 1, 0), 1)],
    [((1, 1, 0), 0), ((1, 1, 0), 1), ((1, -1, 0), 2), ((1, -1, 0), 3)],
    [((0, 0, 1), 0), ((0, 0, 1), 2)],
    [((0, 1, 1), 0), ((1, 0, 1), 0), ((1, 0, 1), 2)],
    [((0, 0, -1), 3)],
    [((0, 1, -1), 1), ((1, 0, -1), 1), ((1, 0, -1), 3)],
    [((0, 0, -1), 3), ((0, 0, -1), 1)],
    [((0, 0, 1), 2), ((0, 0, 1), 0)],
)
SIZES = [len(group) for group in GROUPS]
SLOTS = sum(SIZES)
CORNER = SLOTS - 4
SLOT_OF = {where: i for i, where in enumerate(sum(GROUPS, [])[:CORNER])}


def place(step, k):
    row, col = k // 2 + step[1], k % 2 + step[2]
    return (step[0], row // 2, col // 2), (row % 2) * 2 + col % 2


def beside_device(device, delta):
    x, r = device // NYZ, device % NYZ
    x = (x + delta[0]) % NKX
    y = (r // 4 + delta[1]) % (NYZ // 4)
    g = (GRAY[r % 4] + delta[2]) % KZB
    return x * NYZ + y * 4 + GRAY[g]


def pair_slots(step, corner):
    lower, upper = [], []
    for k in range(4):
        (dx, dy, dz), t = place(step, k)
        if dx and dy and dz:
            lower.append(CORNER + corner)
            upper.append(SLOT_OF[((dx, dy, 0), t)])
        else:
            lower.append(k)
            upper.append(SLOT_OF[((dx, dy, dz), t)])
    return lower, upper


CORNERS = [(1, 1, 1), (1, -1, 1), (1, 1, -1), (1, -1, -1)]
UNIT_SLOTS = [pair_slots(step, 0)[1] for step in UNITS]
TABLE = [pair_slots(step, CORNERS.index(step) if step in CORNERS else 0) for step in DIAGONALS]
CODES = [(s[0] + 1) * 9 + (s[1] + 1) * 3 + s[2] + 1 for s in UNITS + DIAGONALS]


def halves(x):
    hi = x.astype(jnp.bfloat16)
    return hi, (x - hi.astype(jnp.float32)).astype(jnp.bfloat16)


def three(a_hi, a_lo, b_hi, b_lo):
    def dot(a, b):
        return lax.dot_general(a, b, (((1,), (0,)), ((), ())), preferred_element_type=jnp.float32)

    return dot(a_hi, b_hi) + (dot(a_hi, b_lo) + dot(a_lo, b_hi))


VMEM = pl.BlockSpec(memory_space=pltpu.VMEM)
SMEM = pl.BlockSpec(memory_space=pltpu.SMEM)
PARAMS = pltpu.CompilerParams(vmem_limit_bytes=48 * 1024 * 1024)


def mats(n):
    return jax.ShapeDtypeStruct((n, 2, J, J), jnp.float32)


def reals(n):
    return jax.ShapeDtypeStruct((n, J, J), jnp.float32)


def block(ref_hi, ref_lo, at, re, im, sign):
    for ref, part_re, part_im in zip((ref_hi, ref_lo), halves(re), halves(im)):
        ref[at, :J, :J] = part_re
        ref[at, :J, J:] = part_im
        ref[at, J:, :J] = -part_im if sign > 0 else part_im
        ref[at, J:, J:] = part_re if sign > 0 else -part_re


def plan_kernel(offsets, weights, basis, rows, corner_rows, ends, row_data, flipped):
    codes = [(offsets[r, 0] + 1) * 9 + (offsets[r, 1] + 1) * 3 + offsets[r, 2] + 1 for r in range(NB)]
    for j in range(NB):
        rows[j] = 0
    for i in range(3):
        for k in range(4):
            ends[0, i, k] = k
            ends[1, i, k] = k
    count, any_flip = 0, 0
    for i, code in enumerate(CODES):
        row, found, flip = 0, 0, 0
        for r in range(NB):
            along, against = codes[r] == code, codes[r] == 26 - code
            row += jnp.where(along | against, r, 0)
            found += jnp.where(along | against, 1, 0)
            flip += jnp.where(against, 1, 0)
        if i < 3:
            rows[i] = row
            continue
        if DIAGONALS[i - 3] in CORNERS:
            corner_rows[CORNERS.index(DIAGONALS[i - 3])] = row
        place_at = jnp.minimum(count, 2)

        @pl.when(found > 0)
        def _():
            rows[3 + place_at] = row
            lower, upper = TABLE[i - 3]
            for k in range(4):
                ends[0, place_at, k] = jnp.where(flip > 0, upper[k], lower[k])
                ends[1, place_at, k] = jnp.where(flip > 0, lower[k], upper[k])

        count += found
        any_flip += flip
    flipped[0] = any_flip
    for j in range(NB):
        row = rows[j]
        row_data[j, 0] = weights[row]
        for c in range(3):
            step = offsets[row, 0].astype(jnp.float32) * basis[0, c]
            for x in range(1, 3):
                step += offsets[row, x].astype(jnp.float32) * basis[x, c]
            row_data[j, 1 + c] = step


def make_rows(offsets, weights, basis):
    whole = jnp.int32, jnp.float32
    shapes = [((NB,), 0), ((4,), 0), ((2, 3, 4), 0), ((NB, 4), 1), ((1,), 0)]
    return pl.pallas_call(
        plan_kernel,
        in_specs=[SMEM] * 3,
        out_specs=[SMEM] * len(shapes),
        out_shape=[jax.ShapeDtypeStruct(shape, whole[kind]) for shape, kind in shapes],
        name="make_rows",
    )(offsets, weights, basis)


def left_kernel(corner_rows, u_ref, m_ref, v_ref, corner_ref, b_hi, b_lo):
    a_hi, a_lo = halves(jnp.concatenate([u_ref[0, 0].T, u_ref[0, 1].T], 1))
    for j in range(NB):
        block(b_hi, b_lo, j % 2, m_ref[0, j, 0], m_ref[0, j, 1], -1)
        made = three(a_hi, a_lo, b_hi[j % 2], b_lo[j % 2])
        v_ref[0, j, 0] = made[:, :J]
        v_ref[0, j, 1] = made[:, J:]
    corner_ref[0] = v_ref[0, corner_rows[corner_of(pl.program_id(0))]]


def corner_of(k):
    return jnp.where(k == 3, 0, jnp.where(k == 1, 1, jnp.where(k == 2, 2, 3)))


def left_products(corner_rows, own_u, local_m):
    return pl.pallas_call(
        left_kernel,
        grid=(4,),
        in_specs=[
            SMEM,
            pl.BlockSpec((1, 2, J, J), lambda k: (k, 0, 0, 0)),
            pl.BlockSpec((1, NB, 2, J, J), lambda k: (k, 0, 0, 0, 0)),
        ],
        out_specs=[
            pl.BlockSpec((1, NB, 2, J, J), lambda k: (k, 0, 0, 0, 0)),
            pl.BlockSpec((1, 2, J, J), lambda k: (corner_of(k), 0, 0, 0)),
        ],
        scratch_shapes=[
            pltpu.VMEM((2, 2 * J, 2 * J), jnp.bfloat16),
            pltpu.VMEM((2, 2 * J, 2 * J), jnp.bfloat16),
        ],
        out_shape=[jax.ShapeDtypeStruct((4, NB, 2, J, J), jnp.float32), mats(4)],
        compiler_params=PARAMS,
        cost_estimate=pl.CostEstimate(flops=1 << 32, bytes_accessed=8 << 20, transcendentals=0),
        name="left_products",
    )(corner_rows, own_u, local_m)


def write_pair(p_ref, d_ref, at, left_re, left_im, right_re, right_im, b_hi, b_lo):
    a_hi, a_lo = halves(jnp.concatenate([left_re, left_im], 1))
    slot = at % 2
    block(b_hi, b_lo, slot, right_re, right_im, 1)
    made = three(a_hi, a_lo, b_hi[slot], b_lo[slot])
    eye = lax.broadcasted_iota(jnp.int32, (J, J), 0) == lax.broadcasted_iota(jnp.int32, (J, J), 1)
    p_ref[at, 0] = made[:, :J]
    p_ref[at, 1] = made[:, J:]
    j, k = at // 4, at % 4
    d_ref[0, j, k : k + 1, :] = jnp.sum(jnp.where(eye, made[:, :J], 0.0), 0, keepdims=True)
    d_ref[1, j, k : k + 1, :] = jnp.sum(jnp.where(eye, made[:, J:], 0.0), 0, keepdims=True)


def write_phases(row_data, first, d_ref, phase_ref, sums):
    for j in range(3):
        d_re, d_im = d_ref[0, j], d_ref[1, j]
        phase = jnp.arctan2(d_im, d_re)
        phase_ref[j] = phase
        weight = row_data[first + j, 0]
        along = jnp.sum(phase, 0, keepdims=True) * weight
        for c in range(3):
            sums[c] = sums[c] + along * row_data[first + j, 1 + c]
        spread = 1.0 - d_re * d_re - d_im * d_im + phase * phase
        sums[3] = sums[3] + weight * jnp.sum(spread, 0, keepdims=True)
    return jnp.concatenate(sums, 0)


def unit_kernel(rows, row_data, own_ref, x_ref, y_ref, z_ref, v_ref, p_ref, d_ref, phase_ref, sum_ref, b_hi, b_lo):
    found = {i: (own_ref, i) for i in range(4)}
    for ref, slots in ((x_ref, UNIT_SLOTS[0]), (y_ref, UNIT_SLOTS[1][2:]), (z_ref, UNIT_SLOTS[2][1::2])):
        found.update({slot: (ref, i) for i, slot in enumerate(slots)})
    for p in range(12):
        j, k = p // 4, p % 4
        ref, i = found[UNIT_SLOTS[j][k]]
        row = rows[j]
        write_pair(p_ref, d_ref, p, v_ref[k, row, 0], v_ref[k, row, 1], ref[i, 0], ref[i, 1], b_hi, b_lo)
    sum_ref[...] = write_phases(row_data, 0, d_ref, phase_ref, [jnp.zeros((1, J), jnp.float32)] * 4)


def diagonal_kernel(ends, rows, row_data, so_far_ref, *refs, any_sign):
    sizes = SIZES if any_sign else SIZES[:-2]
    parts, rest = refs[: len(sizes)], refs[len(sizes) :]
    if any_sign:
        v_ref, far_ref, *rest = rest
    else:
        v_ref, corner_ref, *rest = rest
    p_ref, d_ref, phase_ref, sum_ref, slots, b_hi, b_lo = rest
    at = 0
    for ref, n in zip(parts, sizes):
        slots[at : at + n] = ref[...]
        at += n
    for p in range(12):
        j, k = p // 4, p % 4
        low, up = ends[0, j, k], ends[1, j, k]
        if any_sign:
            left_re, left_im = far_ref[low, j, 0], far_ref[low, j, 1]
        else:
            row, here = rows[3 + j], low < 4
            own, got = jnp.minimum(low, 3), jnp.maximum(low - CORNER, 0)
            left_re = jnp.where(here, v_ref[own, row, 0], corner_ref[got, 0])
            left_im = jnp.where(here, v_ref[own, row, 1], corner_ref[got, 1])
        write_pair(p_ref, d_ref, p, left_re, left_im, slots[up, 0], slots[up, 1], b_hi, b_lo)
    total = write_phases(row_data, 3, d_ref, phase_ref, [so_far_ref[i : i + 1] for i in range(4)])
    for i in range(NKX):
        sum_ref[i] = total


def product_call(kernel, name, tables, arrays, sum_shape, extra=()):
    return pl.pallas_call(
        kernel,
        in_specs=[SMEM] * len(tables) + [VMEM] * len(arrays),
        out_specs=[VMEM] * 4,
        out_shape=[mats(12)] + [jax.ShapeDtypeStruct(n + (J,), jnp.float32) for n in ((2, 3, 4), (3, 4), sum_shape)],
        scratch_shapes=[
            *extra,
            pltpu.VMEM((2, 2 * J, 2 * J), jnp.bfloat16),
            pltpu.VMEM((2, 2 * J, 2 * J), jnp.bfloat16),
        ],
        compiler_params=PARAMS,
        cost_estimate=pl.CostEstimate(flops=1 << 32, bytes_accessed=4 << 20, transcendentals=0),
        name=name,
    )(*tables, *arrays)


def unit_products(rows, row_data, own, x, y, z, v):
    return product_call(unit_kernel, "unit_products", [rows, row_data], [own, x, y, z, v], (4,))


def diagonal_products(ends, rows, row_data, so_far, parts, v, corner_v, far=None):
    return product_call(
        functools.partial(diagonal_kernel, any_sign=far is not None),
        "diagonal_products",
        [ends, rows, row_data],
        [so_far, *parts, v] + ([corner_v] if far is None else [far]),
        (NKX, 4),
        [pltpu.VMEM((SLOTS, 2, J, J), jnp.float32)],
    )


def plain_and_cross(re, im, a, b):
    return re * a + im * b, im * a - re * b


def term_kernel(ends, row_data, pu_ref, du_ref, phu_ref, pd_ref, dd_ref, phd_ref, got_ref, *refs):
    total_ref, outs = refs[0], refs[1 : 1 + len(SIZES)]
    plain, cross, rows_a, rows_b, turned_a, turned_b = refs[1 + len(SIZES) :]
    total = jnp.sum(got_ref[...], 0)
    total_ref[...] = total
    centres = (-2.0 / NK) * total[:3]
    for j in range(NB):
        along = centres[0:1] * row_data[j, 1]
        for c in range(1, 3):
            along += centres[c : c + 1] * row_data[j, 1 + c]
        d_ref, phase_ref = (du_ref, phu_ref) if j < 3 else (dd_ref, phd_ref)
        d_re, d_im = d_ref[0, j % 3], d_ref[1, j % 3]
        ratio = (phase_ref[j % 3] + along) / (d_re * d_re + d_im * d_im)
        f_re = row_data[j, 0] * (d_re + ratio * d_im)
        f_im = row_data[j, 0] * (ratio * d_re - d_im)
        rows_a[4 * j : 4 * j + 4, :] = f_re + f_im
        rows_b[4 * j : 4 * j + 4, :] = f_re - f_im
    turned_a[...] = rows_a[...].T
    turned_b[...] = rows_b[...].T

    fixed = {slot: [] for slot in range(SLOTS)}
    for p in range(12):
        fixed[p % 4].append((p, True))
        fixed[UNIT_SLOTS[p // 4][p % 4]].append((p, False))
    step = J // 4
    for slot in range(SLOTS):
        for start in range(0, J, step):
            part = slice(start, start + step)
            sums = [jnp.zeros((step, J), jnp.float32)] * 2
            for p, starts_here in fixed[slot]:
                re, im = pu_ref[p, 0, part, :], pu_ref[p, 1, part, :]
                if starts_here:
                    a, b = rows_a[p : p + 1, :], rows_b[p : p + 1, :]
                    one, two = plain_and_cross(re, im, a, b)
                    sums = [sums[0] + one, sums[1] + two]
                else:
                    a, b = turned_a[part, p : p + 1], turned_b[part, p : p + 1]
                    one, two = plain_and_cross(re, im, a, b)
                    sums = [sums[0] - one, sums[1] - two]
            plain[slot, part, :], cross[slot, part, :] = sums
    for p in range(12):
        low, up = ends[0, p // 4, p % 4], ends[1, p // 4, p % 4]
        q = 12 + p
        for start in range(0, J, step):
            part = slice(start, start + step)
            re, im = pd_ref[p, 0, part, :], pd_ref[p, 1, part, :]
            one, two = plain_and_cross(re, im, rows_a[q : q + 1, :], rows_b[q : q + 1, :])
            plain[low, part, :] += one
            cross[low, part, :] += two
            one, two = plain_and_cross(re, im, turned_a[part, q : q + 1], turned_b[part, q : q + 1])
            plain[up, part, :] -= one
            cross[up, part, :] -= two
    at = 0
    for ref, n in zip(outs, SIZES):
        for i in range(n):
            ref[i] = 2.0 * (plain[at] + cross[at].T)
            at += 1


def pair_terms(ends, row_data, unit, diagonal, got):
    return pl.pallas_call(
        term_kernel,
        in_specs=[SMEM, SMEM] + [VMEM] * 7,
        out_specs=[VMEM] * (1 + len(SIZES)),
        out_shape=[jax.ShapeDtypeStruct((4, J), jnp.float32)] + [reals(n) for n in SIZES],
        scratch_shapes=[pltpu.VMEM((SLOTS, J, J), jnp.float32)] * 2 + [pltpu.VMEM((J, J), jnp.float32)] * 4,
        compiler_params=PARAMS,
        cost_estimate=pl.CostEstimate(flops=1 << 24, bytes_accessed=8 << 20, transcendentals=0),
        name="pair_terms",
    )(ends, row_data, *unit, *diagonal, got)


def fold_kernel(own_ref, x_ref, y_ref, y_back_ref, z_ref, z_back_ref, g_ref):
    for k in range(4):
        total = own_ref[k] + x_ref[k]
        total += y_ref[k] if k < 2 else y_back_ref[k - 2]
        if k == 0:
            total += z_ref[0] + z_ref[3]
        elif k == 1:
            total += z_back_ref[2]
        elif k == 2:
            total += z_ref[1] + z_ref[2]
        else:
            total += z_back_ref[0] + z_back_ref[1]
        turned = total.T
        g_ref[k, 0] = 0.5 * (total - turned)
        g_ref[k, 1] = 0.5 * (total + turned)


def fold_terms(*arrays):
    return pl.pallas_call(
        fold_kernel,
        in_specs=[VMEM] * len(arrays),
        out_specs=VMEM,
        out_shape=mats(4),
        compiler_params=PARAMS,
        name="fold_terms",
    )(*arrays)


def fetch(delta, *blocks):
    route = [(beside_device(i, delta), i) for i in range(NKX * NYZ)]
    return lax.ppermute(jnp.concatenate(blocks, 0), AXES, route)


def give_back(delta, block):
    route = [(i, beside_device(i, delta)) for i in range(NKX * NYZ)]
    return lax.ppermute(block, AXES, route)


X, Y, Y_BACK, Z, Z_BACK = (1, 0, 0), (0, 1, 0), (0, -1, 0), (0, 0, 1), (0, 0, -1)


def halo(own):
    y = fetch(Y, own[0:2])
    y_back = fetch(Y_BACK, own[2:4])
    x = fetch(X, own)
    z = fetch(Z, own[0::2])
    z_back = fetch(Z_BACK, own[3:4])
    xy = fetch(X, y, y_back)
    beside = fetch(Z, y[0:1], x[0::2])
    beside_back = fetch(Z_BACK, y[1:2], x[1::2])
    return own, x, y, xy, z, beside, z_back, beside_back


def corners(field):
    return fetch(Z_BACK, field[0:2]), fetch(Z, field[2:4])


def fold_halo(own, x, y, xy, z, beside, z_back, beside_back, corner, corner_back):
    xy = give_back(X, xy)
    beside = give_back(Z, beside)
    beside_back = give_back(Z_BACK, beside_back)
    sides = [beside[1:2], beside_back[1:2], beside[2:3], beside_back[2:3]]
    x = x + jnp.concatenate(sides, 0)
    x, z, corner_back, z_back, corner = lax.optimization_barrier(
        (x, z, corner_back, z_back, corner)
    )
    x = give_back(X, x)
    z = give_back(Z, jnp.concatenate([z, corner_back], 0))
    z_back = give_back(Z_BACK, jnp.concatenate([z_back, corner], 0))
    y = give_back(Y, y + xy[0:2] + jnp.concatenate([beside[0:1], beside_back[0:1]], 0))
    y_back = give_back(Y_BACK, xy[2:4])
    return fold_terms(own, x, y, y_back, z, z_back)


def over_all(copies):
    x = copies[0] + lax.ppermute(copies[0], "kyz", [(i, i ^ 1) for i in range(NYZ)])
    one_core = [[core + 2 * i for i in range(NYZ // 2)] for core in range(2)]
    copies = jnp.broadcast_to(x[None], (NYZ // 2,) + x.shape)
    x = jnp.sum(lax.all_to_all(copies, "kyz", 0, 0, axis_index_groups=one_core), 0)
    copies = jnp.broadcast_to(x[None], (NKX,) + x.shape)
    return lax.all_to_all(copies, "kx", 0, 0)


def on_device(intersections, rotations, offsets, weights, basis):
    own_u = rotations.reshape(4, 2, J, J)
    local_m = intersections.reshape(4, NB, 2, J, J)
    parts = halo(own_u)
    rows, corner_rows, ends, row_data, flipped = make_rows(offsets, weights, basis)
    v, corner_v = left_products(corner_rows, own_u, local_m)
    *unit, so_far = unit_products(rows, row_data, own_u, parts[1], parts[2], parts[4], v)

    corner_v, x, z, z_back = lax.optimization_barrier((corner_v, parts[1], parts[4], parts[6]))
    parts = (parts[0], x, *parts[2:4], z, parts[5], z_back, parts[7])
    corner_v = jnp.concatenate(corners(corner_v), 0)

    def usual(ends, rows, row_data, so_far, v, corner_v, *parts):
        return diagonal_products(ends, rows, row_data, so_far, parts, v, corner_v)

    def any_sign(ends, rows, row_data, so_far, v, corner_v, *parts):
        own_v = jnp.stack([v[:, rows[j]] for j in range(3, NB)], 1)
        own = jnp.concatenate([parts[0][:, None], own_v], 1)
        low = corners(jnp.concatenate([own[3:4], own[1:3], own[0:1]], 0))
        far = jnp.concatenate(halo(own_v) + tuple(block[:, 1:] for block in low), 0)
        parts += tuple(block[:, 0] for block in low)
        return diagonal_products(ends, rows, row_data, so_far, parts, v, corner_v, far)

    *diagonal, part = lax.cond(
        flipped[0] > 0, any_sign, usual, ends, rows, row_data, so_far, v, corner_v, *parts
    )
    got = over_all(part)
    total, *terms = pair_terms(ends, row_data, unit, diagonal, got)
    gradient = fold_halo(*terms)
    centres = (-2.0 / NK) * total[:3]
    spread = (2.0 / NK) * jnp.sum(total[3]) - jnp.sum(centres * centres)
    return gradient.reshape(1, 1, 2, 2, 2, J, J), centres, spread


def solution(mesh):
    placed = (
        P("kx", "kyz", None, None, None, None, None, None),
        P("kx", "kyz", None, None, None, None, None),
        P(),
        P(),
        P(),
    )
    return jax.shard_map(
        on_device,
        mesh=mesh,
        in_specs=placed,
        out_specs=(P("kx", "kyz", None, None, None, None, None), P(), P()),
        check_vma=False,
    )
```

```python
import functools

import jax
import jax.numpy as jnp
from jax import lax
from jax.experimental import pallas as pl
from jax.experimental.pallas import tpu as pltpu
from jax.sharding import PartitionSpec as P

NB = 6
KZB = 4
J = 128
NKX = 8
NYZ = 32
NK = 1024
AXES = ("kx", "kyz")

UNITS = [(1, 0, 0), (0, 1, 0), (0, 0, 1)]
DIAGONALS = [
    (1, 1, 0),
    (1, -1, 0),
    (1, 0, 1),
    (1, 0, -1),
    (0, 1, 1),
    (0, 1, -1),
    (1, 1, 1),
    (1, 1, -1),
    (1, -1, 1),
    (1, -1, -1),
]
GRAY = [0, 1, 3, 2]
GROUPS = (
    [((0, 0, 0), t) for t in range(4)],
    [((1, 0, 0), t) for t in range(4)],
    [((0, 1, 0), 0), ((0, 1, 0), 1)],
    [((1, 1, 0), 0), ((1, 1, 0), 1), ((1, -1, 0), 2), ((1, -1, 0), 3)],
    [((0, 0, 1), 0), ((0, 0, 1), 2)],
    [((0, 1, 1), 0), ((1, 0, 1), 0), ((1, 0, 1), 2)],
    [((0, 0, -1), 3)],
    [((0, 1, -1), 1), ((1, 0, -1), 1), ((1, 0, -1), 3)],
    [((0, 0, -1), 3), ((0, 0, -1), 1)],
    [((0, 0, 1), 2), ((0, 0, 1), 0)],
)
SIZES = [len(group) for group in GROUPS]
SLOTS = sum(SIZES)
CORNER = SLOTS - 4
SLOT_OF = {where: i for i, where in enumerate(sum(GROUPS, [])[:CORNER])}


def place(step, k):
    row, col = k // 2 + step[1], k % 2 + step[2]
    return (step[0], row // 2, col // 2), (row % 2) * 2 + col % 2


def beside_device(device, delta):
    x, r = device // NYZ, device % NYZ
    x = (x + delta[0]) % NKX
    y = (r // 4 + delta[1]) % (NYZ // 4)
    g = (GRAY[r % 4] + delta[2]) % KZB
    return x * NYZ + y * 4 + GRAY[g]


def pair_slots(step, corner):
    lower, upper = [], []
    for k in range(4):
        (dx, dy, dz), t = place(step, k)
        if dx and dy and dz:
            lower.append(CORNER + corner)
            upper.append(SLOT_OF[((dx, dy, 0), t)])
        else:
            lower.append(k)
            upper.append(SLOT_OF[((dx, dy, dz), t)])
    return lower, upper


CORNERS = [(1, 1, 1), (1, -1, 1), (1, 1, -1), (1, -1, -1)]
UNIT_SLOTS = [pair_slots(step, 0)[1] for step in UNITS]
TABLE = [pair_slots(step, CORNERS.index(step) if step in CORNERS else 0) for step in DIAGONALS]
CODES = [(s[0] + 1) * 9 + (s[1] + 1) * 3 + s[2] + 1 for s in UNITS + DIAGONALS]


def halves(x):
    hi = x.astype(jnp.bfloat16)
    return hi, (x - hi.astype(jnp.float32)).astype(jnp.bfloat16)


def three(a_hi, a_lo, b_hi, b_lo):
    def dot(a, b):
        return lax.dot_general(a, b, (((1,), (0,)), ((), ())), preferred_element_type=jnp.float32)

    return dot(a_hi, b_hi) + (dot(a_hi, b_lo) + dot(a_lo, b_hi))


VMEM = pl.BlockSpec(memory_space=pltpu.VMEM)
SMEM = pl.BlockSpec(memory_space=pltpu.SMEM)
PARAMS = pltpu.CompilerParams(vmem_limit_bytes=48 * 1024 * 1024)


def mats(n):
    return jax.ShapeDtypeStruct((n, 2, J, J), jnp.float32)


def reals(n):
    return jax.ShapeDtypeStruct((n, J, J), jnp.float32)


def block(ref_hi, ref_lo, at, re, im, sign):
    for ref, part_re, part_im in zip((ref_hi, ref_lo), halves(re), halves(im)):
        ref[at, :J, :J] = part_re
        ref[at, :J, J:] = part_im
        ref[at, J:, :J] = -part_im if sign > 0 else part_im
        ref[at, J:, J:] = part_re if sign > 0 else -part_re


def plan_kernel(offsets, weights, basis, rows, corner_rows, ends, row_data, flipped):
    codes = [(offsets[r, 0] + 1) * 9 + (offsets[r, 1] + 1) * 3 + offsets[r, 2] + 1 for r in range(NB)]
    for j in range(NB):
        rows[j] = 0
    for i in range(3):
        for k in range(4):
            ends[0, i, k] = k
            ends[1, i, k] = k
    count, any_flip = 0, 0
    for i, code in enumerate(CODES):
        row, found, flip = 0, 0, 0
        for r in range(NB):
            along, against = codes[r] == code, codes[r] == 26 - code
            row += jnp.where(along | against, r, 0)
            found += jnp.where(along | against, 1, 0)
            flip += jnp.where(against, 1, 0)
        if i < 3:
            rows[i] = row
            continue
        if DIAGONALS[i - 3] in CORNERS:
            corner_rows[CORNERS.index(DIAGONALS[i - 3])] = row
        place_at = jnp.minimum(count, 2)

        @pl.when(found > 0)
        def _():
            rows[3 + place_at] = row
            lower, upper = TABLE[i - 3]
            for k in range(4):
                ends[0, place_at, k] = jnp.where(flip > 0, upper[k], lower[k])
                ends[1, place_at, k] = jnp.where(flip > 0, lower[k], upper[k])

        count += found
        any_flip += flip
    flipped[0] = any_flip
    for j in range(NB):
        row = rows[j]
        row_data[j, 0] = weights[row]
        for c in range(3):
            step = offsets[row, 0].astype(jnp.float32) * basis[0, c]
            for x in range(1, 3):
                step += offsets[row, x].astype(jnp.float32) * basis[x, c]
            row_data[j, 1 + c] = step


def make_rows(offsets, weights, basis):
    whole = jnp.int32, jnp.float32
    shapes = [((NB,), 0), ((4,), 0), ((2, 3, 4), 0), ((NB, 4), 1), ((1,), 0)]
    return pl.pallas_call(
        plan_kernel,
        in_specs=[SMEM] * 3,
        out_specs=[SMEM] * len(shapes),
        out_shape=[jax.ShapeDtypeStruct(shape, whole[kind]) for shape, kind in shapes],
        name="make_rows",
    )(offsets, weights, basis)


def left_kernel(corner_rows, u_ref, m_ref, v_ref, corner_ref, b_hi, b_lo):
    a_hi, a_lo = halves(jnp.concatenate([u_ref[0, 0].T, u_ref[0, 1].T], 1))
    for j in range(NB):
        block(b_hi, b_lo, j % 2, m_ref[0, j, 0], m_ref[0, j, 1], -1)
        made = three(a_hi, a_lo, b_hi[j % 2], b_lo[j % 2])
        v_ref[0, j, 0] = made[:, :J]
        v_ref[0, j, 1] = made[:, J:]
    corner_ref[0] = v_ref[0, corner_rows[corner_of(pl.program_id(0))]]


def corner_of(k):
    return jnp.where(k == 3, 0, jnp.where(k == 1, 1, jnp.where(k == 2, 2, 3)))


def left_products(corner_rows, own_u, local_m):
    return pl.pallas_call(
        left_kernel,
        grid=(4,),
        in_specs=[
            SMEM,
            pl.BlockSpec((1, 2, J, J), lambda k: (k, 0, 0, 0)),
            pl.BlockSpec((1, NB, 2, J, J), lambda k: (k, 0, 0, 0, 0)),
        ],
        out_specs=[
            pl.BlockSpec((1, NB, 2, J, J), lambda k: (k, 0, 0, 0, 0)),
            pl.BlockSpec((1, 2, J, J), lambda k: (corner_of(k), 0, 0, 0)),
        ],
        scratch_shapes=[
            pltpu.VMEM((2, 2 * J, 2 * J), jnp.bfloat16),
            pltpu.VMEM((2, 2 * J, 2 * J), jnp.bfloat16),
        ],
        out_shape=[jax.ShapeDtypeStruct((4, NB, 2, J, J), jnp.float32), mats(4)],
        compiler_params=PARAMS,
        cost_estimate=pl.CostEstimate(flops=1 << 32, bytes_accessed=8 << 20, transcendentals=0),
        name="left_products",
    )(corner_rows, own_u, local_m)


def write_pair(p_ref, d_ref, at, left_re, left_im, right_re, right_im, b_hi, b_lo):
    a_hi, a_lo = halves(jnp.concatenate([left_re, left_im], 1))
    slot = at
    block(b_hi, b_lo, slot, right_re, right_im, 1)
    made = three(a_hi, a_lo, b_hi[slot], b_lo[slot])
    eye = lax.broadcasted_iota(jnp.int32, (J, J), 0) == lax.broadcasted_iota(jnp.int32, (J, J), 1)
    p_ref[at, 0] = made[:, :J]
    p_ref[at, 1] = made[:, J:]
    j, k = at // 4, at % 4
    d_ref[0, j, k : k + 1, :] = jnp.sum(jnp.where(eye, made[:, :J], 0.0), 0, keepdims=True)
    d_ref[1, j, k : k + 1, :] = jnp.sum(jnp.where(eye, made[:, J:], 0.0), 0, keepdims=True)


def write_phases(row_data, first, d_ref, phase_ref, sums):
    for j in range(3):
        d_re, d_im = d_ref[0, j], d_ref[1, j]
        phase = jnp.arctan2(d_im, d_re)
        phase_ref[j] = phase
        weight = row_data[first + j, 0]
        along = jnp.sum(phase, 0, keepdims=True) * weight
        for c in range(3):
            sums[c] = sums[c] + along * row_data[first + j, 1 + c]
        spread = 1.0 - d_re * d_re - d_im * d_im + phase * phase
        sums[3] = sums[3] + weight * jnp.sum(spread, 0, keepdims=True)
    return jnp.concatenate(sums, 0)


def unit_kernel(rows, row_data, own_ref, x_ref, y_ref, z_ref, v_ref, p_ref, d_ref, phase_ref, sum_ref, b_hi, b_lo):
    found = {i: (own_ref, i) for i in range(4)}
    for ref, slots in ((x_ref, UNIT_SLOTS[0]), (y_ref, UNIT_SLOTS[1][2:]), (z_ref, UNIT_SLOTS[2][1::2])):
        found.update({slot: (ref, i) for i, slot in enumerate(slots)})
    for p in range(12):
        j, k = p // 4, p % 4
        ref, i = found[UNIT_SLOTS[j][k]]
        row = rows[j]
        write_pair(p_ref, d_ref, p, v_ref[k, row, 0], v_ref[k, row, 1], ref[i, 0], ref[i, 1], b_hi, b_lo)
    sum_ref[...] = write_phases(row_data, 0, d_ref, phase_ref, [jnp.zeros((1, J), jnp.float32)] * 4)


def diagonal_kernel(ends, rows, row_data, so_far_ref, *refs, any_sign):
    sizes = SIZES if any_sign else SIZES[:-2]
    parts, rest = refs[: len(sizes)], refs[len(sizes) :]
    if any_sign:
        v_ref, far_ref, *rest = rest
    else:
        v_ref, corner_ref, *rest = rest
    p_ref, d_ref, phase_ref, sum_ref, slots, b_hi, b_lo = rest
    at = 0
    for ref, n in zip(parts, sizes):
        slots[at : at + n] = ref[...]
        at += n
    for p in range(12):
        j, k = p // 4, p % 4
        low, up = ends[0, j, k], ends[1, j, k]
        if any_sign:
            left_re, left_im = far_ref[low, j, 0], far_ref[low, j, 1]
        else:
            row, here = rows[3 + j], low < 4
            own, got = jnp.minimum(low, 3), jnp.maximum(low - CORNER, 0)
            left_re = jnp.where(here, v_ref[own, row, 0], corner_ref[got, 0])
            left_im = jnp.where(here, v_ref[own, row, 1], corner_ref[got, 1])
        write_pair(p_ref, d_ref, p, left_re, left_im, slots[up, 0], slots[up, 1], b_hi, b_lo)
    total = write_phases(row_data, 3, d_ref, phase_ref, [so_far_ref[i : i + 1] for i in range(4)])
    for i in range(NKX):
        sum_ref[i] = total


def product_call(kernel, name, tables, arrays, sum_shape, extra=()):
    return pl.pallas_call(
        kernel,
        in_specs=[SMEM] * len(tables) + [VMEM] * len(arrays),
        out_specs=[VMEM] * 4,
        out_shape=[mats(12)] + [jax.ShapeDtypeStruct(n + (J,), jnp.float32) for n in ((2, 3, 4), (3, 4), sum_shape)],
        scratch_shapes=[
            *extra,
            pltpu.VMEM((12, 2 * J, 2 * J), jnp.bfloat16),
            pltpu.VMEM((12, 2 * J, 2 * J), jnp.bfloat16),
        ],
        compiler_params=PARAMS,
        cost_estimate=pl.CostEstimate(flops=1 << 32, bytes_accessed=4 << 20, transcendentals=0),
        name=name,
    )(*tables, *arrays)


def unit_products(rows, row_data, own, x, y, z, v):
    return product_call(unit_kernel, "unit_products", [rows, row_data], [own, x, y, z, v], (4,))


def diagonal_products(ends, rows, row_data, so_far, parts, v, corner_v, far=None):
    return product_call(
        functools.partial(diagonal_kernel, any_sign=far is not None),
        "diagonal_products",
        [ends, rows, row_data],
        [so_far, *parts, v] + ([corner_v] if far is None else [far]),
        (NKX, 4),
        [pltpu.VMEM((SLOTS, 2, J, J), jnp.float32)],
    )


def plain_and_cross(re, im, a, b):
    return re * a + im * b, im * a - re * b


def term_kernel(ends, row_data, pu_ref, du_ref, phu_ref, pd_ref, dd_ref, phd_ref, got_ref, *refs):
    total_ref, outs = refs[0], refs[1 : 1 + len(SIZES)]
    plain, cross, rows_a, rows_b, turned_a, turned_b = refs[1 + len(SIZES) :]
    total = jnp.sum(got_ref[...], 0)
    total_ref[...] = total
    centres = (-2.0 / NK) * total[:3]
    for j in range(NB):
        along = centres[0:1] * row_data[j, 1]
        for c in range(1, 3):
            along += centres[c : c + 1] * row_data[j, 1 + c]
        d_ref, phase_ref = (du_ref, phu_ref) if j < 3 else (dd_ref, phd_ref)
        d_re, d_im = d_ref[0, j % 3], d_ref[1, j % 3]
        ratio = (phase_ref[j % 3] + along) / (d_re * d_re + d_im * d_im)
        f_re = row_data[j, 0] * (d_re + ratio * d_im)
        f_im = row_data[j, 0] * (ratio * d_re - d_im)
        rows_a[4 * j : 4 * j + 4, :] = f_re + f_im
        rows_b[4 * j : 4 * j + 4, :] = f_re - f_im
    turned_a[...] = rows_a[...].T
    turned_b[...] = rows_b[...].T

    fixed = {slot: [] for slot in range(SLOTS)}
    for p in range(12):
        fixed[p % 4].append((p, True))
        fixed[UNIT_SLOTS[p // 4][p % 4]].append((p, False))
    step = J // 4
    for slot in range(SLOTS):
        for start in range(0, J, step):
            part = slice(start, start + step)
            sums = [jnp.zeros((step, J), jnp.float32)] * 2
            for p, starts_here in fixed[slot]:
                re, im = pu_ref[p, 0, part, :], pu_ref[p, 1, part, :]
                if starts_here:
                    a, b = rows_a[p : p + 1, :], rows_b[p : p + 1, :]
                    one, two = plain_and_cross(re, im, a, b)
                    sums = [sums[0] + one, sums[1] + two]
                else:
                    a, b = turned_a[part, p : p + 1], turned_b[part, p : p + 1]
                    one, two = plain_and_cross(re, im, a, b)
                    sums = [sums[0] - one, sums[1] - two]
            plain[slot, part, :], cross[slot, part, :] = sums
    for p in range(12):
        low, up = ends[0, p // 4, p % 4], ends[1, p // 4, p % 4]
        q = 12 + p
        for start in range(0, J, step):
            part = slice(start, start + step)
            re, im = pd_ref[p, 0, part, :], pd_ref[p, 1, part, :]
            one, two = plain_and_cross(re, im, rows_a[q : q + 1, :], rows_b[q : q + 1, :])
            plain[low, part, :] += one
            cross[low, part, :] += two
            one, two = plain_and_cross(re, im, turned_a[part, q : q + 1], turned_b[part, q : q + 1])
            plain[up, part, :] -= one
            cross[up, part, :] -= two
    at = 0
    for ref, n in zip(outs, SIZES):
        for i in range(n):
            ref[i] = 2.0 * (plain[at] + cross[at].T)
            at += 1


def pair_terms(ends, row_data, unit, diagonal, got):
    return pl.pallas_call(
        term_kernel,
        in_specs=[SMEM, SMEM] + [VMEM] * 7,
        out_specs=[VMEM] * (1 + len(SIZES)),
        out_shape=[jax.ShapeDtypeStruct((4, J), jnp.float32)] + [reals(n) for n in SIZES],
        scratch_shapes=[pltpu.VMEM((SLOTS, J, J), jnp.float32)] * 2 + [pltpu.VMEM((J, J), jnp.float32)] * 4,
        compiler_params=PARAMS,
        cost_estimate=pl.CostEstimate(flops=1 << 24, bytes_accessed=8 << 20, transcendentals=0),
        name="pair_terms",
    )(ends, row_data, *unit, *diagonal, got)


def fold_kernel(own_ref, x_ref, y_ref, y_back_ref, z_ref, z_back_ref, g_ref):
    for k in range(4):
        total = own_ref[k] + x_ref[k]
        total += y_ref[k] if k < 2 else y_back_ref[k - 2]
        if k == 0:
            total += z_ref[0] + z_ref[3]
        elif k == 1:
            total += z_back_ref[2]
        elif k == 2:
            total += z_ref[1] + z_ref[2]
        else:
            total += z_back_ref[0] + z_back_ref[1]
        turned = total.T
        g_ref[k, 0] = 0.5 * (total - turned)
        g_ref[k, 1] = 0.5 * (total + turned)


def fold_terms(*arrays):
    return pl.pallas_call(
        fold_kernel,
        in_specs=[VMEM] * len(arrays),
        out_specs=VMEM,
        out_shape=mats(4),
        compiler_params=PARAMS,
        name="fold_terms",
    )(*arrays)


def fetch(delta, *blocks):
    route = [(beside_device(i, delta), i) for i in range(NKX * NYZ)]
    return lax.ppermute(jnp.concatenate(blocks, 0), AXES, route)


def give_back(delta, block):
    route = [(i, beside_device(i, delta)) for i in range(NKX * NYZ)]
    return lax.ppermute(block, AXES, route)


X, Y, Y_BACK, Z, Z_BACK = (1, 0, 0), (0, 1, 0), (0, -1, 0), (0, 0, 1), (0, 0, -1)


def halo(own):
    y = fetch(Y, own[0:2])
    y_back = fetch(Y_BACK, own[2:4])
    x = fetch(X, own)
    z = fetch(Z, own[0::2])
    z_back = fetch(Z_BACK, own[3:4])
    xy = fetch(X, y, y_back)
    beside = fetch(Z, y[0:1], x[0::2])
    beside_back = fetch(Z_BACK, y[1:2], x[1::2])
    return own, x, y, xy, z, beside, z_back, beside_back


def corners(field):
    return fetch(Z_BACK, field[0:2]), fetch(Z, field[2:4])


def fold_halo(own, x, y, xy, z, beside, z_back, beside_back, corner, corner_back):
    xy = give_back(X, xy)
    beside = give_back(Z, beside)
    beside_back = give_back(Z_BACK, beside_back)
    sides = [beside[1:2], beside_back[1:2], beside[2:3], beside_back[2:3]]
    x = x + jnp.concatenate(sides, 0)
    x, z, corner_back, z_back, corner = lax.optimization_barrier(
        (x, z, corner_back, z_back, corner)
    )
    x = give_back(X, x)
    z = give_back(Z, jnp.concatenate([z, corner_back], 0))
    z_back = give_back(Z_BACK, jnp.concatenate([z_back, corner], 0))
    y = give_back(Y, y + xy[0:2] + jnp.concatenate([beside[0:1], beside_back[0:1]], 0))
    y_back = give_back(Y_BACK, xy[2:4])
    return fold_terms(own, x, y, y_back, z, z_back)


def over_all(copies):
    x = copies[0] + lax.ppermute(copies[0], "kyz", [(i, i ^ 1) for i in range(NYZ)])
    one_core = [[core + 2 * i for i in range(NYZ // 2)] for core in range(2)]
    copies = jnp.broadcast_to(x[None], (NYZ // 2,) + x.shape)
    x = jnp.sum(lax.all_to_all(copies, "kyz", 0, 0, axis_index_groups=one_core), 0)
    copies = jnp.broadcast_to(x[None], (NKX,) + x.shape)
    return lax.all_to_all(copies, "kx", 0, 0)


def on_device(intersections, rotations, offsets, weights, basis):
    own_u = rotations.reshape(4, 2, J, J)
    local_m = intersections.reshape(4, NB, 2, J, J)
    parts = halo(own_u)
    rows, corner_rows, ends, row_data, flipped = make_rows(offsets, weights, basis)
    v, corner_v = left_products(corner_rows, own_u, local_m)
    *unit, so_far = unit_products(rows, row_data, own_u, parts[1], parts[2], parts[4], v)

    corner_v, x, z, z_back = lax.optimization_barrier((corner_v, parts[1], parts[4], parts[6]))
    parts = (parts[0], x, *parts[2:4], z, parts[5], z_back, parts[7])
    corner_v = jnp.concatenate(corners(corner_v), 0)

    def usual(ends, rows, row_data, so_far, v, corner_v, *parts):
        return diagonal_products(ends, rows, row_data, so_far, parts, v, corner_v)

    def any_sign(ends, rows, row_data, so_far, v, corner_v, *parts):
        own_v = jnp.stack([v[:, rows[j]] for j in range(3, NB)], 1)
        own = jnp.concatenate([parts[0][:, None], own_v], 1)
        low = corners(jnp.concatenate([own[3:4], own[1:3], own[0:1]], 0))
        far = jnp.concatenate(halo(own_v) + tuple(block[:, 1:] for block in low), 0)
        parts += tuple(block[:, 0] for block in low)
        return diagonal_products(ends, rows, row_data, so_far, parts, v, corner_v, far)

    *diagonal, part = lax.cond(
        flipped[0] > 0, any_sign, usual, ends, rows, row_data, so_far, v, corner_v, *parts
    )
    got = over_all(part)
    total, *terms = pair_terms(ends, row_data, unit, diagonal, got)
    gradient = fold_halo(*terms)
    centres = (-2.0 / NK) * total[:3]
    spread = (2.0 / NK) * jnp.sum(total[3]) - jnp.sum(centres * centres)
    return gradient.reshape(1, 1, 2, 2, 2, J, J), centres, spread


def solution(mesh):
    placed = (
        P("kx", "kyz", None, None, None, None, None, None),
        P("kx", "kyz", None, None, None, None, None),
        P(),
        P(),
        P(),
    )
    return jax.shard_map(
        on_device,
        mesh=mesh,
        in_specs=placed,
        out_specs=(P("kx", "kyz", None, None, None, None, None), P(), P()),
        check_vma=False,
    )
```
